32 devices in a mesh: row: 8 (over z, y), col: 4 (over x, core).
Axes of the slice: x: 2, y: 2, z: 4, core: 2. Of those that a mesh axis runs over, the one named last changes fastest.
Arguments:
- trailing_matrix: float32 [2048, 2048], P('row', 'col'), may hold values from -24 to 1024, as said below
- rhs_block: float32 [2048, 128], P('row'), may hold values from -144 to 144
Outputs:
- factored: float32 [2048, 2048], P('row', 'col')
- solved_rhs: float32 [2048, 128], P('row')
The draws below stay inside these ranges and needn't reach their ends.
Inputs may be any that keep to these rules, and one draw needn't show every extreme that they name: `trailing_matrix`: symmetric in logical order; its leading 2 * 256 by 512 logical block is positive definite.
All inputs are finite; a program needn't handle non-finite values.
Results may differ from the reference program's by a relative error of at most 0.00011.
Values sent between devices are 32-bit elements; how exact they have to be, the bound alone decides.
A program may use at most 64 MiB of HBM per device.

```python
import jax
import jax.numpy as jnp
from jax import lax

NB = 256
NR = 128
TROW = 1
TCOL = 2
M = 2048
N_ROW = 8
N_COL = 4


def stored_logical(total_len, tiles_dev, parts_count):
    stored = jnp.arange(total_len, dtype=jnp.int32)
    tile_pos = stored // NB
    return (tile_pos // tiles_dev + parts_count * (tile_pos % tiles_dev)) * NB + stored % NB


def draw_trailing_matrix(key, part):
    keys = jax.random.split(key, 3)
    lead_len = 2 * NB
    index_all = jnp.arange(M, dtype=jnp.int32)
    noise = jnp.clip(jax.random.normal(keys[0], (M, M), jnp.float32), -6.0, 6.0)
    upper = index_all[:, None] <= index_all[None, :]
    noise = jnp.where(upper, noise, noise.T)
    in_lead = index_all < lead_len
    boxed = jax.random.uniform(keys[1], (M, M), jnp.float32, -1.0, 1.0)
    boxed = jnp.where(upper, boxed, boxed.T)
    diag_vals = lead_len * (1.0 + jax.random.uniform(keys[2], (M,), jnp.float32, 0.1, 1.0))
    edge = in_lead[:, None] != in_lead[None, :]
    outer = jnp.clip(noise * jnp.where(edge, 4.0, 1.0), -24.0, 24.0)
    both_lead = in_lead[:, None] & in_lead[None, :]
    logical = jnp.where(both_lead, boxed, outer)
    on_diag = (index_all[:, None] == index_all[None, :]) & both_lead
    logical = jnp.where(on_diag, diag_vals[:, None], logical)
    rows_map = stored_logical(M, TROW, N_ROW)
    cols_map = stored_logical(M, TCOL, N_COL)
    return jnp.take(jnp.take(logical, rows_map, axis=0), cols_map, axis=1)


def draw_rhs_block(key, part):
    index_all = jnp.arange(M, dtype=jnp.int32)
    noise = jnp.clip(jax.random.normal(key, (M, NR), jnp.float32), -6.0, 6.0)
    row_scale = jnp.where(index_all < 2 * NB, 24.0, 1.0)
    logical = noise * row_scale[:, None]
    rows_map = stored_logical(M, TROW, N_ROW)
    return jnp.take(logical, rows_map, axis=0)


def setup_inputs(seed: int = 0) -> dict:
    key_list = jax.random.split(jax.random.key(seed), 3)
    return {
        "trailing_matrix": draw_trailing_matrix(jax.random.fold_in(key_list[2], 71), 0),
        "rhs_block": draw_rhs_block(jax.random.fold_in(key_list[2], 71), 0),
    }


def logical_to_stored(total_len, tiles_dev, parts_count):
    logical = jnp.arange(total_len, dtype=jnp.int32)
    tile_pos = logical // NB
    return (tile_pos % parts_count * tiles_dev + tile_pos // parts_count) * NB + logical % NB

def stored_to_logical(total_len, tiles_dev, parts_count):
    stored = jnp.arange(total_len, dtype=jnp.int32)
    tile_pos = stored // NB
    return (tile_pos // tiles_dev + parts_count * (tile_pos % tiles_dev)) * NB + stored % NB

def reference(trailing_matrix, rhs_block):
    highest = lax.Precision.HIGHEST
    row_take = logical_to_stored(M, TROW, N_ROW)
    col_take = logical_to_stored(M, TCOL, N_COL)
    work = jnp.take(jnp.take(trailing_matrix, row_take, axis=0), col_take, axis=1)
    right = jnp.take(rhs_block, row_take, axis=0)
    result = jnp.zeros_like(work)
    for section in range(2):
        start_pos = section * NB
        end_pos = start_pos + NB
        factor = jnp.linalg.cholesky(work[start_pos:end_pos, start_pos:end_pos])
        below_rows = jax.scipy.linalg.solve_triangular(factor, work[end_pos:, start_pos:end_pos].T, lower=True).T
        solved = jax.scipy.linalg.solve_triangular(factor, right[start_pos:end_pos], lower=True)
        right = right.at[start_pos:end_pos].set(solved)
        right = right.at[end_pos:].set(right[end_pos:] - jnp.dot(below_rows, solved, precision=highest))
        work = work.at[end_pos:, end_pos:].set(work[end_pos:, end_pos:] - jnp.dot(below_rows, below_rows.T, precision=highest))
        result = result.at[start_pos:end_pos, start_pos:end_pos].set(factor)
        result = result.at[end_pos:, start_pos:end_pos].set(below_rows)
    result = result.at[2 * NB:, 2 * NB:].set(work[2 * NB:, 2 * NB:])
    row_back = stored_to_logical(M, TROW, N_ROW)
    col_back = stored_to_logical(M, TCOL, N_COL)
    factored = jnp.take(jnp.take(result, row_back, axis=0), col_back, axis=1)
    solved_rhs = jnp.take(right, row_back, axis=0)
    return (factored, solved_rhs)
```

```python
import functools

import jax
import jax.numpy as jnp
from jax import lax
from jax.experimental import pallas as pl
from jax.experimental.pallas import tpu as pltpu
from jax.sharding import PartitionSpec as P

NB = 256
HB = 128
LEAD = 2 * NB
MESH = pl.DeviceIdType.MESH
highest = lax.Precision.HIGHEST


def dot(a, b):
    return jnp.dot(a, b, precision=highest, preferred_element_type=jnp.float32)


def dot_nt(a, b):
    return lax.dot_general(
        a, b, (((1,), (1,)), ((), ())), precision=highest, preferred_element_type=jnp.float32
    )


def exchange_kernel(
    n_row, n_col, a_ref, b_ref, rows_ref, lead_ref, cols_ref, rhs_ref, send_sem, recv_sem
):
    r = lax.axis_index("row")
    c = lax.axis_index("col")

    def at(axis, index):
        return (index, c) if axis == "row" else (r, index)

    axes = (("row", r, n_row), ("col", c, n_col))
    barrier = pltpu.get_barrier_semaphore()
    for axis, me, size in axes:
        pl.semaphore_signal(barrier, inc=1, device_id=at(axis, me + 1 - 2 * (me % 2)), device_id_type=MESH)

        @pl.when(me + 2 < size)
        def _():
            pl.semaphore_signal(barrier, inc=1, device_id=at(axis, me + 2), device_id_type=MESH)

        @pl.when(me >= 2)
        def _():
            pl.semaphore_signal(barrier, inc=1, device_id=at(axis, me - 2), device_id_type=MESH)

    peers = 2
    for axis, me, size in axes:
        peers += (me + 2 < size).astype(jnp.int32) + (me >= 2).astype(jnp.int32)
    pl.semaphore_wait(barrier, peers)

    def copy(ref, item, way, axis, target):
        return pltpu.make_async_remote_copy(
            src_ref=ref,
            dst_ref=ref,
            send_sem=send_sem.at[item, way],
            recv_sem=recv_sem.at[item],
            device_id=at(axis, target),
            device_id_type=MESH,
        )

    def forward(ref, item, axis, parity):
        _, me, size = axes[0] if axis == "row" else axes[1]

        @pl.when(jnp.logical_or(me % 2 != parity, me >= 2))
        def _():
            copy(ref, item, 0, axis, me).wait_recv()

        @pl.when(me % 2 == parity)
        def _():
            @pl.when(me + 2 < size)
            def _():
                copy(ref, item, 0, axis, me + 2).start()

            copy(ref, item, 1, axis, me + 1 - 2 * (me % 2)).start()

    def finish(ref, item, axis, parity):
        _, me, size = axes[0] if axis == "row" else axes[1]

        @pl.when(me % 2 == parity)
        def _():
            @pl.when(me + 2 < size)
            def _():
                copy(ref, item, 0, axis, me + 2).wait_send()

            copy(ref, item, 1, axis, me + 1 - 2 * (me % 2)).wait_send()

    for q in range(2):

        @pl.when(c == q)
        def _():
            rows_ref[q] = a_ref[:, :NB]

        @pl.when(r == q)
        def _():
            cols_ref[q] = a_ref[...]
            rhs_ref[q] = b_ref[...]

    halves = [pl.ds(0, HB), pl.ds(HB, HB)]
    across = [(rows_ref.at[q, half], "col", q) for half in halves for q in range(2)]
    down = [
        (lead_ref.at[0, halves[0]], "row", 0),
        (lead_ref.at[0, halves[1]], "row", 0),
        (lead_ref.at[1], "row", 0),
        (lead_ref.at[2], "row", 1),
    ]
    down += [(cols_ref.at[q, half], "row", q) for half in halves for q in range(2)]
    down += [(rhs_ref.at[q], "row", q) for q in range(2)]

    for item, (ref, axis, parity) in enumerate(across):
        forward(ref, item, axis, parity)

    @pl.when(r == 0)
    def _():
        lead_ref[0] = rows_ref[0]
        lead_ref[1] = rows_ref[1]

    @pl.when(r == 1)
    def _():
        lead_ref[2] = rows_ref[1]

    for item, (ref, axis, parity) in enumerate(down):
        forward(ref, item + len(across), axis, parity)
    for item, (ref, axis, parity) in enumerate(across + down):
        finish(ref, item, axis, parity)


EXCHANGE_ITEMS = 14


def exchange(n_row, n_col, a, b):
    vmem = pl.BlockSpec(memory_space=pltpu.VMEM)
    shapes = [(2, NB, NB), (3, NB, NB), (2,) + a.shape, (2,) + b.shape]
    return pl.pallas_call(
        functools.partial(exchange_kernel, n_row, n_col),
        out_shape=[jax.ShapeDtypeStruct(s, jnp.float32) for s in shapes],
        in_specs=[vmem] * 2,
        out_specs=[vmem] * 4,
        scratch_shapes=[
            pltpu.SemaphoreType.DMA((EXCHANGE_ITEMS, 2)),
            pltpu.SemaphoreType.DMA((EXCHANGE_ITEMS,)),
        ],
        compiler_params=pltpu.CompilerParams(
            collective_id=0, has_side_effects=True, vmem_limit_bytes=40 * 1024 * 1024
        ),
    )(a, b)


def rows_of(x, j):
    return jnp.broadcast_to(x[j : j + 1, :], x.shape)


def invert_factor(s):
    sub = lax.broadcasted_iota(jnp.int32, (8, HB), 0)
    lane = lax.broadcasted_iota(jnp.int32, (8, HB), 1)
    groups = len(s)
    t = [jnp.where(lane == sub + 8 * h, 1.0, 0.0).astype(jnp.float32) for h in range(groups)]
    done = []
    for g in range(groups):
        p, q, f = s[g], t[g], t[g]
        lanes = [jnp.broadcast_to(p[:, 8 * g + k : 8 * g + k + 1], (8, HB)) for k in range(8)]
        scale = jnp.ones((8, HB), jnp.float32)
        for j in range(8):
            here = sub == j
            pivot = rows_of(lanes[j], j)
            inv = 1.0 / pivot
            m = lanes[j] * inv
            for k in range(j + 1, 8):
                row = rows_of(lanes[k], j)
                lanes[k] = jnp.where(here, row * inv, lanes[k] - m * row)
            row = rows_of(p, j)
            p = jnp.where(here, row * inv, p - m * row)
            row = rows_of(q, j)
            q = jnp.where(here, row * inv, q - m * row)
            f = jnp.where(sub > j, f - m * rows_of(f, j), f)
            scale = jnp.where(here, pivot, scale)
        root = lax.rsqrt(scale)
        root = root * (1.5 - 0.5 * scale * root * root)
        done.append(f * root)
        if g + 1 < groups:
            prow = [rows_of(p, k) for k in range(8)]
            qrow = [rows_of(q, k) for k in range(8)]
        for h in range(g + 1, groups):
            lane_cols = [
                jnp.broadcast_to(s[h][:, 8 * g + k : 8 * g + k + 1], (8, HB)) for k in range(8)
            ]
            ps = [lane_cols[k] * prow[k] for k in range(8)]
            qs = [lane_cols[k] * qrow[k] for k in range(8)]
            s[h] = s[h] - (((ps[0] + ps[1]) + (ps[2] + ps[3])) + ((ps[4] + ps[5]) + (ps[6] + ps[7])))
            t[h] = t[h] - (((qs[0] + qs[1]) + (qs[2] + qs[3])) + ((qs[4] + qs[5]) + (qs[6] + qs[7])))
    return done


def factor_lead(s_ref, inv_ref):
    blocks = LEAD // HB

    def step(kb, carry):
        base = pl.multiple_of(kb * HB, HB)
        groups = [
            s_ref[pl.ds(pl.multiple_of(base + 8 * g, 8), 8), pl.ds(base, HB)] for g in range(HB // 8)
        ]
        li = jnp.concatenate(invert_factor(groups), axis=0)
        inv_ref[pl.ds(base, HB), pl.ds(base, HB)] = li
        for k in range(blocks):

            @pl.when(kb == k)
            def _():
                lo, hi = k * HB, (k + 1) * HB
                if k > 0:
                    inv_ref[lo:hi, :lo] = dot(li, inv_ref[lo:hi, :lo])
                if k + 1 < blocks:
                    u = dot(li, s_ref[lo:hi, hi:])
                    ut = u.T
                    s_ref[hi:, hi:] -= dot(ut, u)
                    inv_ref[hi:, :hi] -= dot(ut, inv_ref[lo:hi, :hi])

        return carry

    lax.fori_loop(0, blocks, step, 0)


def compute_kernel(
    n_col, a_ref, b_ref, rows_ref, lead_ref, cols_ref, rhs_ref, out_ref, y_ref, s_ref, inv_ref
):
    r = lax.axis_index("row")
    c = lax.axis_index("col")
    s_ref[:NB, :NB] = lead_ref[0]
    s_ref[:NB, NB:] = lead_ref[1]
    s_ref[NB:, NB:] = lead_ref[2]
    inv_ref[...] = jnp.zeros_like(inv_ref)
    factor_lead(s_ref, inv_ref)

    panels = []
    for k in range(2):
        inv_rows = inv_ref[k * NB : (k + 1) * NB, : (k + 1) * NB]
        total = dot_nt(rows_ref[0], inv_rows[:, :NB])
        if k == 1:
            total += dot_nt(rows_ref[1], inv_rows[:, NB:])
        panels.append(total)
    tri = lax.broadcasted_iota(jnp.int32, (NB, NB), 0) >= lax.broadcasted_iota(jnp.int32, (NB, NB), 1)

    def solve(ref, cols):
        first = dot(inv_ref[:NB, :NB], ref[0, :, cols])
        second = dot(inv_ref[NB:, :NB], ref[0, :, cols]) + dot(inv_ref[NB:, NB:], ref[1, :, cols])
        return first, second

    y0, y1 = solve(rhs_ref, slice(None))
    updated = b_ref[...] - (dot(panels[0], y0) + dot(panels[1], y1))
    y_ref[...] = jnp.where(r == 0, y0, jnp.where(r == 1, y1, updated))
    for slot in range(a_ref.shape[1] // NB):
        cols = slice(slot * NB, (slot + 1) * NB)
        j = c + n_col * slot
        z0, z1 = solve(cols_ref, cols)
        inner = a_ref[:, cols] - (dot(panels[0], z0) + dot(panels[1], z1))
        inner = jnp.where(r >= 2, inner, 0.0)
        if slot == 0:
            panel = jnp.where(j == 0, panels[0], panels[1])
            keep = jnp.logical_or(r > j, jnp.logical_and(r == j, tri))
            inner = jnp.where(j >= 2, inner, jnp.where(keep, panel, 0.0))
        out_ref[:, cols] = inner


def compute(n_col, a, b, rows, lead, cols, rhs):
    vmem = pl.BlockSpec(memory_space=pltpu.VMEM)
    return pl.pallas_call(
        functools.partial(compute_kernel, n_col),
        out_shape=[jax.ShapeDtypeStruct(x.shape, jnp.float32) for x in (a, b)],
        in_specs=[vmem] * 6,
        out_specs=[vmem] * 2,
        scratch_shapes=[
            pltpu.VMEM((LEAD, LEAD), jnp.float32),
            pltpu.VMEM((LEAD, LEAD), jnp.float32),
        ],
        compiler_params=pltpu.CompilerParams(vmem_limit_bytes=40 * 1024 * 1024),
    )(a, b, rows, lead, cols, rhs)


def solution(mesh):
    n_row, n_col = mesh.shape["row"], mesh.shape["col"]

    def per_device(a, b):
        return tuple(compute(n_col, a, b, *exchange(n_row, n_col, a, b)))

    placed = (P("row", "col"), P("row", None))
    return jax.shard_map(
        per_device, mesh=mesh, in_specs=placed, out_specs=placed, check_vma=False
    )
```

```python
import functools

import jax
import jax.numpy as jnp
from jax import lax
from jax.experimental import pallas as pl
from jax.experimental.pallas import tpu as pltpu
from jax.sharding import PartitionSpec as P

NB = 256
HB = 128
LEAD = 2 * NB
MESH = pl.DeviceIdType.MESH
highest = lax.Precision.HIGHEST


def dot(a, b):
    return jnp.dot(a, b, precision=highest, preferred_element_type=jnp.float32)


def dot_nt(a, b):
    return lax.dot_general(
        a, b, (((1,), (1,)), ((), ())), precision=highest, preferred_element_type=jnp.float32
    )


class Exchange:
    def __init__(self, n_row, n_col, send_sem, recv_sem):
        self.r = lax.axis_index("row")
        self.c = lax.axis_index("col")
        self.axes = {"row": (self.r, n_row), "col": (self.c, n_col)}
        self.send_sem, self.recv_sem = send_sem, recv_sem
        self.started = []

    def at(self, axis, index):
        return (index, self.c) if axis == "row" else (self.r, index)

    def barrier(self):
        barrier = pltpu.get_barrier_semaphore()
        peers = 0
        for axis, (me, size) in self.axes.items():
            for there, target in (
                (None, me + 1 - 2 * (me % 2)),
                (me + 2 < size, me + 2),
                (me >= 2, me - 2),
            ):

                def signal():
                    pl.semaphore_signal(
                        barrier, inc=1, device_id=self.at(axis, target), device_id_type=MESH
                    )

                if there is None:
                    signal()
                    peers += 1
                else:
                    pl.when(there)(signal)
                    peers += there.astype(jnp.int32)
        pl.semaphore_wait(barrier, peers)

    def copy(self, ref, item, way, axis, target):
        return pltpu.make_async_remote_copy(
            src_ref=ref,
            dst_ref=ref,
            send_sem=self.send_sem.at[item, way],
            recv_sem=self.recv_sem.at[item],
            device_id=self.at(axis, target),
            device_id_type=MESH,
        )

    def forward(self, ref, axis, parity):
        me, size = self.axes[axis]
        item = len(self.started)
        self.started.append((ref, axis, parity))

        def run_send():
            @pl.when(me + 2 < size)
            def _():
                self.copy(ref, item, 0, axis, me + 2).start()

            self.copy(ref, item, 1, axis, me + 1 - 2 * (me % 2)).start()

        def from_source():
            @pl.when(me == parity)
            def _():
                run_send()

        def elsewhere():
            @pl.when(me != parity)
            def _():
                self.copy(ref, item, 0, axis, me).wait_recv()

                @pl.when(me % 2 == parity)
                def _():
                    run_send()

        return from_source, elsewhere

    def finish(self):
        for item, (ref, axis, parity) in enumerate(self.started):
            me, size = self.axes[axis]

            @pl.when(me % 2 == parity)
            def _():
                @pl.when(me + 2 < size)
                def _():
                    self.copy(ref, item, 0, axis, me + 2).wait_send()

                self.copy(ref, item, 1, axis, me + 1 - 2 * (me % 2)).wait_send()


LEAD_CHUNK = 64
ITEMS = 64
POINTS = 4


def plan_exchange(ex, a_ref, b_ref, rows_ref, lead_ref, cols_ref, rhs_ref):
    r, c = ex.r, ex.c
    width = a_ref.shape[1]
    rows_items = [ex.forward(rows_ref.at[q], "col", q) for q in range(2)]
    first = {}
    lead = {}
    chunks = NB // LEAD_CHUNK
    for k in range(chunks):
        part = pl.ds(k * LEAD_CHUNK, LEAD_CHUNK)
        for q in range(2):
            first[k, q] = ex.forward(cols_ref.at[q, part, pl.ds(0, NB)], "row", q)
        for n, owner in ((0, 0), (1, 1), (2, 1)):
            lead[k, n] = ex.forward(lead_ref.at[n, part], "col", owner)
    rest = [
        [
            ex.forward(cols_ref.at[q, pl.ds(h * HB, HB), pl.ds(NB, width - NB)], "row", q)
            for q in range(2)
        ]
        for h in range(2)
    ]
    rhs_items = [ex.forward(rhs_ref.at[q], "row", q) for q in range(2)]

    def start():
        for q in range(2):

            @pl.when(c == q)
            def _():
                rows_ref[q] = a_ref[:, :NB]

            @pl.when(r == q)
            def _():
                cols_ref[q] = a_ref[...]
                rhs_ref[q] = b_ref[...]

        for k in range(chunks):
            for q in range(2):
                first[k, q][0]()
        for item in rows_items:
            item[0]()
        for pair in rest:
            for item in pair:
                item[0]()
        for item in rhs_items:
            item[0]()

    def first_part(k):
        part = pl.ds(k * LEAD_CHUNK, LEAD_CHUNK)
        for q in range(2):
            first[k, q][1]()

            @pl.when(c == q)
            def _():
                lead_ref[q, part] = cols_ref[0, part, :NB]

            lead[k, q][0]()

        @pl.when(c == 1)
        def _():
            lead_ref[2, part] = cols_ref[1, part, :NB]

        lead[k, 2][0]()

    def lead_part(k):
        for n in range(3):
            lead[k, n][1]()

    def both(items):
        for item in items:
            item[1]()

    ahead = [start, lambda: first_part(0), lambda: first_part(1), lambda: lead_part(0), lambda: lead_part(1)]
    inside = {
        0: [lambda: first_part(2)],
        1: [lambda: first_part(3), lambda: lead_part(2)],
        2: [lambda: lead_part(3)],
        3: [lambda: both(rest[0])],
        4: [lambda: both(rows_items)],
        5: [lambda: both(rest[1])],
        7: [lambda: both(rhs_items)],
    }
    return ahead, inside


def rows_of(x, j):
    return jnp.broadcast_to(x[j : j + 1, :], x.shape)


def invert_factor(s, hook=lambda point: None):
    sub = lax.broadcasted_iota(jnp.int32, (8, HB), 0)
    lane = lax.broadcasted_iota(jnp.int32, (8, HB), 1)
    groups = len(s)
    t = [jnp.where(lane == sub + 8 * h, 1.0, 0.0).astype(jnp.float32) for h in range(groups)]
    done = []
    for g in range(groups):
        if g % (groups // POINTS) == 0:
            hook(g // (groups // POINTS))
        p, q, f = s[g], t[g], t[g]
        lanes = [jnp.broadcast_to(p[:, 8 * g + k : 8 * g + k + 1], (8, HB)) for k in range(8)]
        scale = jnp.ones((8, HB), jnp.float32)
        for j in range(8):
            here = sub == j
            pivot = rows_of(lanes[j], j)
            inv = 1.0 / pivot
            m = lanes[j] * inv
            for k in range(j + 1, 8):
                row = rows_of(lanes[k], j)
                lanes[k] = jnp.where(here, row * inv, lanes[k] - m * row)
            row = rows_of(p, j)
            p = jnp.where(here, row * inv, p - m * row)
            row = rows_of(q, j)
            q = jnp.where(here, row * inv, q - m * row)
            f = jnp.where(sub > j, f - m * rows_of(f, j), f)
            scale = jnp.where(here, pivot, scale)
        root = lax.rsqrt(scale)
        root = root * (1.5 - 0.5 * scale * root * root)
        done.append(f * root)
        if g + 1 < groups:
            prow = [rows_of(p, k) for k in range(8)]
            qrow = [rows_of(q, k) for k in range(8)]
        for h in range(g + 1, groups):
            lane_cols = [
                jnp.broadcast_to(s[h][:, 8 * g + k : 8 * g + k + 1], (8, HB)) for k in range(8)
            ]
            ps = [lane_cols[k] * prow[k] for k in range(8)]
            qs = [lane_cols[k] * qrow[k] for k in range(8)]
            s[h] = s[h] - (((ps[0] + ps[1]) + (ps[2] + ps[3])) + ((ps[4] + ps[5]) + (ps[6] + ps[7])))
            t[h] = t[h] - (((qs[0] + qs[1]) + (qs[2] + qs[3])) + ((qs[4] + qs[5]) + (qs[6] + qs[7])))
    return done


def factor_lead(lead_ref, s_ref, inv_ref, inside):
    blocks = LEAD // HB

    def step(kb, carry):
        def hook(point):
            for k in range(blocks):
                jobs = inside.get(k * POINTS + point)
                if jobs:

                    @pl.when(kb == k)
                    def _():
                        for job in jobs:
                            job()

        base = pl.multiple_of(kb * HB, HB)
        for k in range(blocks):

            @pl.when(kb == k)
            def _():
                rows = slice(k * HB, (k + 1) * HB)
                here = slice(k * HB % NB, k * HB % NB + HB)
                if k * HB < NB:
                    s_ref[rows, :NB] += lead_ref[0, here]
                    s_ref[rows, NB:] += lead_ref[1, here]
                else:
                    s_ref[rows, NB:] += lead_ref[2, here]

        groups = [
            s_ref[pl.ds(pl.multiple_of(base + 8 * g, 8), 8), pl.ds(base, HB)] for g in range(HB // 8)
        ]
        li = jnp.concatenate(invert_factor(groups, hook), axis=0)
        inv_ref[pl.ds(base, HB), pl.ds(base, HB)] = li
        for k in range(blocks):

            @pl.when(kb == k)
            def _():
                lo, hi = k * HB, (k + 1) * HB
                if k > 0:
                    inv_ref[lo:hi, :lo] = dot(li, inv_ref[lo:hi, :lo])
                if k + 1 < blocks:
                    u = dot(li, s_ref[lo:hi, hi:])
                    ut = u.T
                    s_ref[hi:, hi:] -= dot(ut, u)
                    inv_ref[hi:, :hi] -= dot(ut, inv_ref[lo:hi, :hi])

        return carry

    lax.fori_loop(0, blocks, step, 0)


def whole_kernel(
    n_row,
    n_col,
    a_ref,
    b_ref,
    out_ref,
    y_ref,
    rows_ref,
    lead_ref,
    cols_ref,
    rhs_ref,
    s_ref,
    inv_ref,
    send_sem,
    recv_sem,
):
    ex = Exchange(n_row, n_col, send_sem, recv_sem)
    r, c = ex.r, ex.c
    ex.barrier()
    ahead, inside = plan_exchange(ex, a_ref, b_ref, rows_ref, lead_ref, cols_ref, rhs_ref)
    ahead[0]()
    s_ref[...] = jnp.zeros_like(s_ref)
    inv_ref[...] = jnp.zeros_like(inv_ref)
    for job in ahead[1:]:
        job()
    factor_lead(lead_ref, s_ref, inv_ref, inside)

    panels = []
    for k in range(2):
        inv_rows = inv_ref[k * NB : (k + 1) * NB, : (k + 1) * NB]
        total = dot_nt(rows_ref[0], inv_rows[:, :NB])
        if k == 1:
            total += dot_nt(rows_ref[1], inv_rows[:, NB:])
        panels.append(total)
    tri = lax.broadcasted_iota(jnp.int32, (NB, NB), 0) >= lax.broadcasted_iota(jnp.int32, (NB, NB), 1)

    def solve(ref, cols):
        first = dot(inv_ref[:NB, :NB], ref[0, :, cols])
        second = dot(inv_ref[NB:, :NB], ref[0, :, cols]) + dot(inv_ref[NB:, NB:], ref[1, :, cols])
        return first, second

    y0, y1 = solve(rhs_ref, slice(None))
    updated = b_ref[...] - (dot(panels[0], y0) + dot(panels[1], y1))
    y_ref[...] = jnp.where(r == 0, y0, jnp.where(r == 1, y1, updated))
    for slot in range(a_ref.shape[1] // NB):
        cols = slice(slot * NB, (slot + 1) * NB)
        j = c + n_col * slot
        z0, z1 = solve(cols_ref, cols)
        inner = a_ref[:, cols] - (dot(panels[0], z0) + dot(panels[1], z1))
        inner = jnp.where(r >= 2, inner, 0.0)
        if slot == 0:
            panel = jnp.where(j == 0, panels[0], panels[1])
            keep = jnp.logical_or(r > j, jnp.logical_and(r == j, tri))
            inner = jnp.where(j >= 2, inner, jnp.where(keep, panel, 0.0))
        out_ref[:, cols] = inner
    ex.finish()


def whole(n_row, n_col, a, b):
    vmem = pl.BlockSpec(memory_space=pltpu.VMEM)
    shapes = [(2, NB, NB), (3, NB, NB), (2,) + a.shape, (2,) + b.shape, (LEAD, LEAD), (LEAD, LEAD)]
    return pl.pallas_call(
        functools.partial(whole_kernel, n_row, n_col),
        out_shape=[jax.ShapeDtypeStruct(x.shape, jnp.float32) for x in (a, b)],
        in_specs=[vmem] * 2,
        out_specs=[vmem] * 2,
        scratch_shapes=[pltpu.VMEM(s, jnp.float32) for s in shapes]
        + [pltpu.SemaphoreType.DMA((ITEMS, 2)), pltpu.SemaphoreType.DMA((ITEMS,))],
        compiler_params=pltpu.CompilerParams(
            collective_id=0, has_side_effects=True, vmem_limit_bytes=40 * 1024 * 1024
        ),
    )(a, b)


def solution(mesh):
    n_row, n_col = mesh.shape["row"], mesh.shape["col"]

    def per_device(a, b):
        return tuple(whole(n_row, n_col, a, b))

    placed = (P("row", "col"), P("row", None))
    return jax.shard_map(
        per_device, mesh=mesh, in_specs=placed, out_specs=placed, check_vma=False
    )
```

```python
import functools

import jax
import jax.numpy as jnp
from jax import lax
from jax.experimental import pallas as pl
from jax.experimental.pallas import tpu as pltpu
from jax.sharding import PartitionSpec as P

NB = 256
HB = 128
LEAD = 2 * NB
MESH = pl.DeviceIdType.MESH
highest = lax.Precision.HIGHEST


def dot(a, b):
    return jnp.dot(a, b, precision=highest, preferred_element_type=jnp.float32)


def dot_nt(a, b):
    return lax.dot_general(
        a, b, (((1,), (1,)), ((), ())), precision=highest, preferred_element_type=jnp.float32
    )


class Exchange:
    def __init__(self, n_row, n_col, send_sem, recv_sem):
        self.r = lax.axis_index("row")
        self.c = lax.axis_index("col")
        self.axes = {"row": (self.r, n_row), "col": (self.c, n_col)}
        self.send_sem, self.recv_sem = send_sem, recv_sem
        self.items = 0
        self.sent = []

    def at(self, axis, index):
        return (index, self.c) if axis == "row" else (self.r, index)

    def barrier(self):
        barrier = pltpu.get_barrier_semaphore()
        peers = 0
        for axis, (me, size) in self.axes.items():
            for there, target in (
                (None, me + 1 - 2 * (me % 2)),
                (me + 2 < size, me + 2),
                (me >= 2, me - 2),
            ):

                def signal():
                    pl.semaphore_signal(
                        barrier, inc=1, device_id=self.at(axis, target), device_id_type=MESH
                    )

                if there is None:
                    signal()
                    peers += 1
                else:
                    pl.when(there)(signal)
                    peers += there.astype(jnp.int32)
        pl.semaphore_wait(barrier, peers)

    def copy(self, ref, item, way, axis, target):
        return pltpu.make_async_remote_copy(
            src_ref=ref,
            dst_ref=ref,
            send_sem=self.send_sem.at[item, way],
            recv_sem=self.recv_sem.at[item],
            device_id=self.at(axis, target),
            device_id_type=MESH,
        )

    def flow(self, ref, axis, source, low=0, active=True):
        me, size = self.axes[axis]
        item = self.items
        self.items += 1
        chain = jnp.logical_and(active, me % 2 == source % 2)
        sends = (
            (jnp.logical_and(chain, jnp.logical_and(me >= source, me + 2 < size)), me + 2),
            (jnp.logical_and(chain, jnp.logical_and(me <= source, me >= low + 2)), me - 2),
            (chain, me + 1 - 2 * (me % 2)),
        )

        def send():
            for way, (there, target) in enumerate(sends):

                @pl.when(there)
                def _():
                    self.copy(ref, item, way, axis, target).start()

        def wait_sent():
            for way, (there, target) in enumerate(sends):

                @pl.when(there)
                def _():
                    self.copy(ref, item, way, axis, target).wait_send()

        self.sent.append(wait_sent)

        def from_source():
            @pl.when(jnp.logical_and(active, me == source))
            def _():
                send()

        def elsewhere():
            @pl.when(jnp.logical_and(active, me != source))
            def _():
                self.copy(ref, item, 2, axis, me + 1 - 2 * (me % 2)).wait_recv()
                send()

        return from_source, elsewhere

    def finish(self):
        for wait_sent in self.sent:
            wait_sent()


ITEMS = 48
POINTS = 4
BLOCKS = LEAD // HB
UPPER = [(i, j) for i in range(BLOCKS) for j in range(i, BLOCKS)]
LEAD_ITEMS = [(0, 1, 0, 0), (1, 1, 0, 0), (2, 2, 0, 1), (4, 1, 0, 0), (5, 2, 0, 1), (7, 3, 1, 1)]


def plan_exchange(ex, n_col, slots, a_ref, b_ref, rows_ref, lead_ref, pan_ref, rhs_ref):
    r, c = ex.r, ex.c
    halves = [pl.ds(0, HB), pl.ds(HB, HB)]
    rows_items = [ex.flow(rows_ref.at[q], "col", q) for q in range(2)]
    lead = []
    for start, count, q, owner in LEAD_ITEMS:
        ref = lead_ref.at[pl.ds(start, count)]
        lead.append((ex.flow(ref, "row", q, active=c == owner), ex.flow(ref, "col", owner)))
    rhs = [
        (ex.flow(rhs_ref.at[q], "row", q, active=c == 2), ex.flow(rhs_ref.at[q], "col", 2))
        for q in range(2)
    ]
    pan = []
    for q in range(2):
        for half in halves:
            for t in range(slots):
                j = c + n_col * t
                active = jnp.logical_and(r >= 2, j >= 2)
                pan.append(ex.flow(pan_ref.at[t, q, half], "row", j, low=2, active=active))

    def start():
        for n, (i, j) in enumerate(UPPER):
            q, owner = i * HB // NB, j * HB // NB

            @pl.when(jnp.logical_and(r == q, c == owner))
            def _():
                lead_ref[n] = a_ref[i * HB % NB : i * HB % NB + HB, j * HB % NB : j * HB % NB + HB]

        for row_flow, _ in lead:
            row_flow[0]()
        for q in range(2):

            @pl.when(c == q)
            def _():
                rows_ref[q] = a_ref[:, :NB]

            rows_items[q][0]()

            @pl.when(jnp.logical_and(r == q, c == 2))
            def _():
                rhs_ref[q] = b_ref[...]

            rhs[q][0][0]()

    def pass_on(pair):
        pair[0][1]()
        pair[1][0]()

    def start_pan():
        for t in range(slots):

            @pl.when(jnp.logical_and(r >= 2, r == c + n_col * t))
            def _():
                pan_ref[t] = rows_ref[...]

        for item in pan:
            item[0]()

    inside = {}

    def put(point, *jobs):
        inside.setdefault(point, []).extend(jobs)

    def along_row(n):
        return lambda: pass_on(lead[n])

    def along_col(n):
        return lead[n][1][1]

    ahead = [start, along_row(0), along_col(0)]
    put(0, along_row(1), along_row(2))
    put(1, along_col(1), along_col(2), rows_items[0][1], rows_items[1][1], start_pan)
    put(2, along_row(3), along_row(4))
    put(3, along_col(3), along_col(4))
    put(4, along_row(5))
    put(5, along_col(5))
    put(6, lambda: pass_on(rhs[0]), lambda: pass_on(rhs[1]))
    put(8, rhs[0][1][1], rhs[1][1][1])
    for n, item in enumerate(pan):
        put(5 + n * 8 // len(pan), item[1])
    return ahead, inside


def rows_of(x, j):
    return jnp.broadcast_to(x[j : j + 1, :], x.shape)


def invert_factor(s, hook=lambda point: None):
    sub = lax.broadcasted_iota(jnp.int32, (8, HB), 0)
    lane = lax.broadcasted_iota(jnp.int32, (8, HB), 1)
    groups = len(s)
    t = [jnp.where(lane == sub + 8 * h, 1.0, 0.0).astype(jnp.float32) for h in range(groups)]
    done = []
    for g in range(groups):
        if g % (groups // POINTS) == 0:
            hook(g // (groups // POINTS))
        p, q, f = s[g], t[g], t[g]
        lanes = [jnp.broadcast_to(p[:, 8 * g + k : 8 * g + k + 1], (8, HB)) for k in range(8)]
        scale = jnp.ones((8, HB), jnp.float32)
        for j in range(8):
            here = sub == j
            pivot = rows_of(lanes[j], j)
            inv = 1.0 / pivot
            m = lanes[j] * inv
            for k in range(j + 1, 8):
                row = rows_of(lanes[k], j)
                lanes[k] = jnp.where(here, row * inv, lanes[k] - m * row)
            row = rows_of(p, j)
            p = jnp.where(here, row * inv, p - m * row)
            row = rows_of(q, j)
            q = jnp.where(here, row * inv, q - m * row)
            f = jnp.where(sub > j, f - m * rows_of(f, j), f)
            scale = jnp.where(here, pivot, scale)
        root = lax.rsqrt(scale)
        root = root * (1.5 - 0.5 * scale * root * root)
        done.append(f * root)
        if g + 1 < groups:
            prow = [rows_of(p, k) for k in range(8)]
            qrow = [rows_of(q, k) for k in range(8)]
        for h in range(g + 1, groups):
            lane_cols = [
                jnp.broadcast_to(s[h][:, 8 * g + k : 8 * g + k + 1], (8, HB)) for k in range(8)
            ]
            ps = [lane_cols[k] * prow[k] for k in range(8)]
            qs = [lane_cols[k] * qrow[k] for k in range(8)]
            s[h] = s[h] - (((ps[0] + ps[1]) + (ps[2] + ps[3])) + ((ps[4] + ps[5]) + (ps[6] + ps[7])))
            t[h] = t[h] - (((qs[0] + qs[1]) + (qs[2] + qs[3])) + ((qs[4] + qs[5]) + (qs[6] + qs[7])))
    return done


def factor_lead(lead_ref, s_ref, inv_ref, inside):
    blocks = BLOCKS

    def step(kb, carry):
        def hook(point):
            for k in range(blocks):
                jobs = inside.get(k * POINTS + point)
                if jobs:

                    @pl.when(kb == k)
                    def _():
                        for job in jobs:
                            job()

        base = pl.multiple_of(kb * HB, HB)
        for k in range(blocks):

            @pl.when(kb == k)
            def _():
                rows = slice(k * HB, (k + 1) * HB)
                s_ref[rows, rows] += lead_ref[UPPER.index((k, k))]

        groups = [
            s_ref[pl.ds(pl.multiple_of(base + 8 * g, 8), 8), pl.ds(base, HB)] for g in range(HB // 8)
        ]
        li = jnp.concatenate(invert_factor(groups, hook), axis=0)
        inv_ref[pl.ds(base, HB), pl.ds(base, HB)] = li
        for k in range(blocks):

            @pl.when(kb == k)
            def _():
                lo, hi = k * HB, (k + 1) * HB
                if k > 0:
                    inv_ref[lo:hi, :lo] = dot(li, inv_ref[lo:hi, :lo])
                for j in range(k + 1, blocks):
                    s_ref[lo:hi, j * HB : (j + 1) * HB] += lead_ref[UPPER.index((k, j))]
                if k + 1 < blocks:
                    u = dot(li, s_ref[lo:hi, hi:])
                    ut = u.T
                    s_ref[hi:, hi:] -= dot(ut, u)
                    inv_ref[hi:, :hi] -= dot(ut, inv_ref[lo:hi, :hi])

        return carry

    lax.fori_loop(0, blocks, step, 0)


def whole_kernel(
    n_row,
    n_col,
    a_ref,
    b_ref,
    out_ref,
    y_ref,
    rows_ref,
    lead_ref,
    pan_ref,
    rhs_ref,
    s_ref,
    inv_ref,
    send_sem,
    recv_sem,
):
    slots = a_ref.shape[1] // NB
    ex = Exchange(n_row, n_col, send_sem, recv_sem)
    r, c = ex.r, ex.c
    ex.barrier()
    ahead, inside = plan_exchange(
        ex, n_col, slots, a_ref, b_ref, rows_ref, lead_ref, pan_ref, rhs_ref
    )
    ahead[0]()
    s_ref[...] = jnp.zeros_like(s_ref)
    inv_ref[...] = jnp.zeros_like(inv_ref)
    for job in ahead[1:]:
        job()
    factor_lead(lead_ref, s_ref, inv_ref, inside)

    def panel(first, second):
        left = dot_nt(first, inv_ref[:NB, :NB])
        right = dot_nt(first, inv_ref[NB:, :NB]) + dot_nt(second, inv_ref[NB:, NB:])
        return left, right

    p0, p1 = panel(rows_ref[0], rows_ref[1])
    y0 = dot(inv_ref[:NB, :NB], rhs_ref[0])
    y1 = dot(inv_ref[NB:, :NB], rhs_ref[0]) + dot(inv_ref[NB:, NB:], rhs_ref[1])
    updated = b_ref[...] - (dot(p0, y0) + dot(p1, y1))
    y_ref[...] = jnp.where(r == 0, y0, jnp.where(r == 1, y1, updated))
    tri = lax.broadcasted_iota(jnp.int32, (NB, NB), 0) >= lax.broadcasted_iota(jnp.int32, (NB, NB), 1)
    for slot in range(slots):
        cols = slice(slot * NB, (slot + 1) * NB)
        j = c + n_col * slot
        inner = jnp.logical_and(r >= 2, j >= 2)

        @pl.when(inner)
        def _():
            z0, z1 = panel(pan_ref[slot, 0], pan_ref[slot, 1])
            out_ref[:, cols] = a_ref[:, cols] - (dot_nt(p0, z0) + dot_nt(p1, z1))

        @pl.when(jnp.logical_not(inner))
        def _():
            keep = jnp.logical_or(r > j, jnp.logical_and(r == j, tri))
            out_ref[:, cols] = jnp.where(keep, jnp.where(j == 0, p0, p1), 0.0)

    ex.finish()


def whole(n_row, n_col, a, b):
    vmem = pl.BlockSpec(memory_space=pltpu.VMEM)
    shapes = [
        (2, NB, NB),
        (len(UPPER), HB, HB),
        (a.shape[1] // NB, 2, NB, NB),
        (2,) + b.shape,
        (LEAD, LEAD),
        (LEAD, LEAD),
    ]
    return pl.pallas_call(
        functools.partial(whole_kernel, n_row, n_col),
        out_shape=[jax.ShapeDtypeStruct(x.shape, jnp.float32) for x in (a, b)],
        in_specs=[vmem] * 2,
        out_specs=[vmem] * 2,
        scratch_shapes=[pltpu.VMEM(s, jnp.float32) for s in shapes]
        + [pltpu.SemaphoreType.DMA((ITEMS, 3)), pltpu.SemaphoreType.DMA((ITEMS,))],
        compiler_params=pltpu.CompilerParams(
            collective_id=0, has_side_effects=True, vmem_limit_bytes=40 * 1024 * 1024
        ),
    )(a, b)


def solution(mesh):
    n_row, n_col = mesh.shape["row"], mesh.shape["col"]

    def per_device(a, b):
        return tuple(whole(n_row, n_col, a, b))

    placed = (P("row", "col"), P("row", None))
    return jax.shard_map(
        per_device, mesh=mesh, in_specs=placed, out_specs=placed, check_vma=False
    )
```

```python
import functools

import jax
import jax.numpy as jnp
from jax import lax
from jax.experimental import pallas as pl
from jax.experimental.pallas import tpu as pltpu
from jax.sharding import PartitionSpec as P

NB = 256
HB = 128
LEAD = 2 * NB
MESH = pl.DeviceIdType.MESH
highest = lax.Precision.HIGHEST


def dot(a, b):
    return jnp.dot(a, b, precision=highest, preferred_element_type=jnp.float32)


def dot_nt(a, b):
    return lax.dot_general(
        a, b, (((1,), (1,)), ((), ())), precision=highest, preferred_element_type=jnp.float32
    )


class Exchange:
    def __init__(self, n_row, n_col, send_sem, recv_sem):
        self.r = lax.axis_index("row")
        self.c = lax.axis_index("col")
        self.axes = {"row": (self.r, n_row), "col": (self.c, n_col)}
        self.send_sem, self.recv_sem = send_sem, recv_sem
        self.items = 0
        self.sent = []

    def at(self, axis, index):
        return (index, self.c) if axis == "row" else (self.r, index)

    def barrier(self):
        barrier = pltpu.get_barrier_semaphore()
        peers = 0
        for axis, (me, size) in self.axes.items():
            for there, target in (
                (None, me + 1 - 2 * (me % 2)),
                (me + 2 < size, me + 2),
                (me >= 2, me - 2),
            ):

                def signal():
                    pl.semaphore_signal(
                        barrier, inc=1, device_id=self.at(axis, target), device_id_type=MESH
                    )

                if there is None:
                    signal()
                    peers += 1
                else:
                    pl.when(there)(signal)
                    peers += there.astype(jnp.int32)
        pl.semaphore_wait(barrier, peers)

    def copy(self, ref, item, way, axis, target):
        return pltpu.make_async_remote_copy(
            src_ref=ref,
            dst_ref=ref,
            send_sem=self.send_sem.at[item, way],
            recv_sem=self.recv_sem.at[item],
            device_id=self.at(axis, target),
            device_id_type=MESH,
        )

    def flow(self, ref, axis, source, low=0, active=True):
        me, size = self.axes[axis]
        item = self.items
        self.items += 1
        chain = jnp.logical_and(active, me % 2 == source % 2)
        sends = (
            (jnp.logical_and(chain, jnp.logical_and(me >= source, me + 2 < size)), me + 2),
            (jnp.logical_and(chain, jnp.logical_and(me <= source, me >= low + 2)), me - 2),
            (chain, me + 1 - 2 * (me % 2)),
        )

        def send():
            for way, (there, target) in enumerate(sends):

                @pl.when(there)
                def _():
                    self.copy(ref, item, way, axis, target).start()

        def wait_sent():
            for way, (there, target) in enumerate(sends):

                @pl.when(there)
                def _():
                    self.copy(ref, item, way, axis, target).wait_send()

        self.sent.append(wait_sent)

        def from_source():
            @pl.when(jnp.logical_and(active, me == source))
            def _():
                send()

        def elsewhere():
            @pl.when(jnp.logical_and(active, me != source))
            def _():
                self.copy(ref, item, 2, axis, me + 1 - 2 * (me % 2)).wait_recv()
                send()

        return from_source, elsewhere

    def swap(self, src, dst, landing, active_out, active_in):
        item = self.items
        self.items += 1
        pair = self.c + 1 - 2 * (self.c % 2)

        def send():
            @pl.when(active_out)
            def _():
                descriptor(src, dst).start()

        def receive():
            @pl.when(active_in)
            def _():
                descriptor(landing, landing).wait_recv()

        def descriptor(here, there):
            return pltpu.make_async_remote_copy(
                src_ref=here,
                dst_ref=there,
                send_sem=self.send_sem.at[item, 0],
                recv_sem=self.recv_sem.at[item],
                device_id=self.at("col", pair),
                device_id_type=MESH,
            )

        def wait_sent():
            @pl.when(active_out)
            def _():
                descriptor(src, dst).wait_send()

        self.sent.append(wait_sent)
        return send, receive

    def finish(self):
        for wait_sent in self.sent:
            wait_sent()


ITEMS = 48
POINTS = 4
BLOCKS = LEAD // HB
UPPER = [(i, j) for i in range(BLOCKS) for j in range(i, BLOCKS)]
LEAD_ITEMS = [(0, 1, 0, 0), (1, 1, 0, 0), (2, 2, 0, 1), (4, 1, 0, 0), (5, 2, 0, 1), (7, 3, 1, 1)]


def plan_exchange(ex, n_col, slots, a_ref, b_ref, rows_ref, lead_ref, pan_ref, car_ref, rhs_ref):
    r, c = ex.r, ex.c
    halves = [pl.ds(0, HB), pl.ds(HB, HB)]
    rows_early = [ex.flow(rows_ref.at[q], "col", q, active=r >= 2) for q in range(2)]
    rows_late = [ex.flow(rows_ref.at[q], "col", q, active=r < 2) for q in range(2)]
    lead = []
    for start, count, q, owner in LEAD_ITEMS:
        ref = lead_ref.at[pl.ds(start, count)]
        lead.append((ex.flow(ref, "row", q, active=c == owner), ex.flow(ref, "col", owner)))
    rhs = [
        (ex.flow(rhs_ref.at[q], "row", q, active=c == 2), ex.flow(rhs_ref.at[q], "col", 2))
        for q in range(2)
    ]
    q = c % 2
    pair = c + 1 - 2 * q
    pan = []
    for half in halves:
        for t in range(slots):
            j, j_pair = c + n_col * t, pair + n_col * t
            own = jnp.logical_and(r >= 2, j >= 2)
            other = jnp.logical_and(r >= 2, j_pair >= 2)
            pan.append(
                (
                    ex.flow(pan_ref.at[t, q, half], "row", j, low=2, active=own),
                    ex.flow(car_ref.at[t, half], "row", j_pair, low=2, active=other),
                    ex.swap(
                        car_ref.at[t, half],
                        pan_ref.at[t, q, half],
                        pan_ref.at[t, 1 - q, half],
                        jnp.logical_and(other, r != j_pair),
                        jnp.logical_and(own, r != j),
                    ),
                )
            )

    def start():
        for n, (i, j) in enumerate(UPPER):
            q, owner = i * HB // NB, j * HB // NB

            @pl.when(jnp.logical_and(r == q, c == owner))
            def _():
                lead_ref[n] = a_ref[i * HB % NB : i * HB % NB + HB, j * HB % NB : j * HB % NB + HB]

        for row_flow, _ in lead:
            row_flow[0]()
        for q in range(2):

            @pl.when(c == q)
            def _():
                rows_ref[q] = a_ref[:, :NB]

            rows_early[q][0]()

            @pl.when(jnp.logical_and(r == q, c == 2))
            def _():
                rhs_ref[q] = b_ref[...]

            rhs[q][0][0]()

    def pass_on(pair):
        pair[0][1]()
        pair[1][0]()

    def start_pan(native):
        here = jnp.logical_and(r >= 2, c < 2 if native else c >= 2)
        for t in range(slots):

            @pl.when(jnp.logical_and(here, r == c + n_col * t))
            def _():
                pan_ref[t, q] = a_ref[:, :NB] if native else rows_ref[q]

            @pl.when(jnp.logical_and(here, r == pair + n_col * t))
            def _():
                car_ref[t] = a_ref[:, :NB] if native else rows_ref[q]

        @pl.when(here)
        def _():
            for own, other, _ in pan:
                own[0]()
                other[0]()

    def own_pan():
        for t in range(slots):

            @pl.when(jnp.logical_and(r >= 2, r == c + n_col * t))
            def _():
                pan_ref[t, 1 - q] = rows_ref[1 - q]

    def pan_row(n):
        def run():
            own, other, swap = pan[n]
            own[1]()
            other[1]()
            swap[0]()

        return run

    inside = {}

    def put(point, *jobs):
        inside.setdefault(point, []).extend(jobs)

    def along_row(n):
        return lambda: pass_on(lead[n])

    def along_col(n):
        return lead[n][1][1]

    ahead = [start, lambda: start_pan(True), along_row(0), along_col(0)]
    put(0, along_row(1), along_row(2))
    put(1, along_col(1), along_col(2), rows_early[0][1], rows_early[1][1])
    put(1, lambda: start_pan(False), own_pan)
    put(2, along_row(3), along_row(4))
    put(3, along_col(3), along_col(4))
    put(4, along_row(5))
    put(5, along_col(5))
    put(6, lambda: pass_on(rhs[0]), lambda: pass_on(rhs[1]))
    put(8, rhs[0][1][1], rhs[1][1][1])
    put(5, rows_late[0][0], rows_late[1][0])
    put(10, rows_late[0][1], rows_late[1][1])
    for n, item in enumerate(pan):
        at = 5 + n * 8 // len(pan)
        put(at, pan_row(n))
        put(at + 3, item[2][1])
    return ahead, inside


def rows_of(x, j):
    return jnp.broadcast_to(x[j : j + 1, :], x.shape)


def invert_factor(s, hook=lambda point: None):
    sub = lax.broadcasted_iota(jnp.int32, (8, HB), 0)
    lane = lax.broadcasted_iota(jnp.int32, (8, HB), 1)
    groups = len(s)
    t = [jnp.where(lane == sub + 8 * h, 1.0, 0.0).astype(jnp.float32) for h in range(groups)]
    done = []
    for g in range(groups):
        if g % (groups // POINTS) == 0:
            hook(g // (groups // POINTS))
        p, q, f = s[g], t[g], t[g]
        lanes = [jnp.broadcast_to(p[:, 8 * g + k : 8 * g + k + 1], (8, HB)) for k in range(8)]
        scale = jnp.ones((8, HB), jnp.float32)
        for j in range(8):
            here = sub == j
            pivot = rows_of(lanes[j], j)
            inv = 1.0 / pivot
            m = lanes[j] * inv
            for k in range(j + 1, 8):
                row = rows_of(lanes[k], j)
                lanes[k] = jnp.where(here, row * inv, lanes[k] - m * row)
            row = rows_of(p, j)
            p = jnp.where(here, row * inv, p - m * row)
            row = rows_of(q, j)
            q = jnp.where(here, row * inv, q - m * row)
            f = jnp.where(sub > j, f - m * rows_of(f, j), f)
            scale = jnp.where(here, pivot, scale)
        root = lax.rsqrt(scale)
        root = root * (1.5 - 0.5 * scale * root * root)
        done.append(f * root)
        if g + 1 < groups:
            prow = [rows_of(p, k) for k in range(8)]
            qrow = [rows_of(q, k) for k in range(8)]
        for h in range(g + 1, groups):
            lane_cols = [
                jnp.broadcast_to(s[h][:, 8 * g + k : 8 * g + k + 1], (8, HB)) for k in range(8)
            ]
            ps = [lane_cols[k] * prow[k] for k in range(8)]
            qs = [lane_cols[k] * qrow[k] for k in range(8)]
            s[h] = s[h] - (((ps[0] + ps[1]) + (ps[2] + ps[3])) + ((ps[4] + ps[5]) + (ps[6] + ps[7])))
            t[h] = t[h] - (((qs[0] + qs[1]) + (qs[2] + qs[3])) + ((qs[4] + qs[5]) + (qs[6] + qs[7])))
    return done


def factor_lead(lead_ref, s_ref, inv_ref, inside):
    blocks = BLOCKS

    def step(kb, carry):
        def hook(point):
            for k in range(blocks):
                jobs = inside.get(k * POINTS + point)
                if jobs:

                    @pl.when(kb == k)
                    def _():
                        for job in jobs:
                            job()

        base = pl.multiple_of(kb * HB, HB)
        for k in range(blocks):

            @pl.when(kb == k)
            def _():
                rows = slice(k * HB, (k + 1) * HB)
                s_ref[rows, rows] += lead_ref[UPPER.index((k, k))]

        groups = [
            s_ref[pl.ds(pl.multiple_of(base + 8 * g, 8), 8), pl.ds(base, HB)] for g in range(HB // 8)
        ]
        li = jnp.concatenate(invert_factor(groups, hook), axis=0)
        inv_ref[pl.ds(base, HB), pl.ds(base, HB)] = li
        for k in range(blocks):

            @pl.when(kb == k)
            def _():
                lo, hi = k * HB, (k + 1) * HB
                if k > 0:
                    inv_ref[lo:hi, :lo] = dot(li, inv_ref[lo:hi, :lo])
                for j in range(k + 1, blocks):
                    s_ref[lo:hi, j * HB : (j + 1) * HB] += lead_ref[UPPER.index((k, j))]
                if k + 1 < blocks:
                    u = dot(li, s_ref[lo:hi, hi:])
                    ut = u.T
                    s_ref[hi:, hi:] -= dot(ut, u)
                    inv_ref[hi:, :hi] -= dot(ut, inv_ref[lo:hi, :hi])

        return carry

    lax.fori_loop(0, blocks, step, 0)


def whole_kernel(
    n_row,
    n_col,
    a_ref,
    b_ref,
    out_ref,
    y_ref,
    rows_ref,
    lead_ref,
    pan_ref,
    car_ref,
    rhs_ref,
    s_ref,
    inv_ref,
    send_sem,
    recv_sem,
):
    slots = a_ref.shape[1] // NB
    ex = Exchange(n_row, n_col, send_sem, recv_sem)
    r, c = ex.r, ex.c
    ex.barrier()
    ahead, inside = plan_exchange(
        ex, n_col, slots, a_ref, b_ref, rows_ref, lead_ref, pan_ref, car_ref, rhs_ref
    )
    ahead[0]()
    s_ref[...] = jnp.zeros_like(s_ref)
    inv_ref[...] = jnp.zeros_like(inv_ref)
    for job in ahead[1:]:
        job()
    factor_lead(lead_ref, s_ref, inv_ref, inside)

    def panel(first, second):
        left = dot_nt(first, inv_ref[:NB, :NB])
        right = dot_nt(first, inv_ref[NB:, :NB]) + dot_nt(second, inv_ref[NB:, NB:])
        return left, right

    p0, p1 = panel(rows_ref[0], rows_ref[1])
    y0 = dot(inv_ref[:NB, :NB], rhs_ref[0])
    y1 = dot(inv_ref[NB:, :NB], rhs_ref[0]) + dot(inv_ref[NB:, NB:], rhs_ref[1])
    updated = b_ref[...] - (dot(p0, y0) + dot(p1, y1))
    y_ref[...] = jnp.where(r == 0, y0, jnp.where(r == 1, y1, updated))
    tri = lax.broadcasted_iota(jnp.int32, (NB, NB), 0) >= lax.broadcasted_iota(jnp.int32, (NB, NB), 1)
    for slot in range(slots):
        cols = slice(slot * NB, (slot + 1) * NB)
        j = c + n_col * slot
        inner = jnp.logical_and(r >= 2, j >= 2)

        @pl.when(inner)
        def _():
            z0, z1 = panel(pan_ref[slot, 0], pan_ref[slot, 1])
            out_ref[:, cols] = a_ref[:, cols] - (dot_nt(p0, z0) + dot_nt(p1, z1))

        @pl.when(jnp.logical_not(inner))
        def _():
            keep = jnp.logical_or(r > j, jnp.logical_and(r == j, tri))
            out_ref[:, cols] = jnp.where(keep, jnp.where(j == 0, p0, p1), 0.0)

    ex.finish()


def whole(n_row, n_col, a, b):
    vmem = pl.BlockSpec(memory_space=pltpu.VMEM)
    shapes = [
        (2, NB, NB),
        (len(UPPER), HB, HB),
        (a.shape[1] // NB, 2, NB, NB),
        (a.shape[1] // NB, NB, NB),
        (2,) + b.shape,
        (LEAD, LEAD),
        (LEAD, LEAD),
    ]
    return pl.pallas_call(
        functools.partial(whole_kernel, n_row, n_col),
        out_shape=[jax.ShapeDtypeStruct(x.shape, jnp.float32) for x in (a, b)],
        in_specs=[vmem] * 2,
        out_specs=[vmem] * 2,
        scratch_shapes=[pltpu.VMEM(s, jnp.float32) for s in shapes]
        + [pltpu.SemaphoreType.DMA((ITEMS, 3)), pltpu.SemaphoreType.DMA((ITEMS,))],
        compiler_params=pltpu.CompilerParams(
            collective_id=0, has_side_effects=True, vmem_limit_bytes=40 * 1024 * 1024
        ),
    )(a, b)


def solution(mesh):
    n_row, n_col = mesh.shape["row"], mesh.shape["col"]

    def per_device(a, b):
        return tuple(whole(n_row, n_col, a, b))

    placed = (P("row", "col"), P("row", None))
    return jax.shard_map(
        per_device, mesh=mesh, in_specs=placed, out_specs=placed, check_vma=False
    )
```

```python
import functools

import jax
import jax.numpy as jnp
from jax import lax
from jax.experimental import pallas as pl
from jax.experimental.pallas import tpu as pltpu
from jax.sharding import PartitionSpec as P

NB = 256
HB = 128
LEAD = 2 * NB
MESH = pl.DeviceIdType.MESH
highest = lax.Precision.HIGHEST


def dot(a, b):
    return jnp.dot(a, b, precision=highest, preferred_element_type=jnp.float32)


def dot_nt(a, b):
    return lax.dot_general(
        a, b, (((1,), (1,)), ((), ())), precision=highest, preferred_element_type=jnp.float32
    )


class Exchange:
    def __init__(self, n_row, n_col, send_sem, recv_sem):
        self.r = lax.axis_index("row")
        self.c = lax.axis_index("col")
        self.axes = {"row": (self.r, n_row), "col": (self.c, n_col)}
        self.send_sem, self.recv_sem = send_sem, recv_sem
        self.items = 0
        self.sent = []

    def at(self, axis, index):
        return (index, self.c) if axis == "row" else (self.r, index)

    def barrier(self):
        barrier = pltpu.get_barrier_semaphore()
        peers = 0
        for axis, (me, size) in self.axes.items():
            for there, target in (
                (None, me + 1 - 2 * (me % 2)),
                (me + 2 < size, me + 2),
                (me >= 2, me - 2),
            ):

                def signal():
                    pl.semaphore_signal(
                        barrier, inc=1, device_id=self.at(axis, target), device_id_type=MESH
                    )

                if there is None:
                    signal()
                    peers += 1
                else:
                    pl.when(there)(signal)
                    peers += there.astype(jnp.int32)
        pl.semaphore_wait(barrier, peers)

    def copy(self, ref, item, way, axis, target):
        return pltpu.make_async_remote_copy(
            src_ref=ref,
            dst_ref=ref,
            send_sem=self.send_sem.at[item, way],
            recv_sem=self.recv_sem.at[item],
            device_id=self.at(axis, target),
            device_id_type=MESH,
        )

    def flow(self, ref, axis, source, low=0, active=True):
        me, size = self.axes[axis]
        item = self.items
        self.items += 1
        chain = jnp.logical_and(active, me % 2 == source % 2)
        sends = (
            (jnp.logical_and(chain, jnp.logical_and(me >= source, me + 2 < size)), me + 2),
            (jnp.logical_and(chain, jnp.logical_and(me <= source, me >= low + 2)), me - 2),
            (chain, me + 1 - 2 * (me % 2)),
        )

        def send():
            for way, (there, target) in enumerate(sends):

                @pl.when(there)
                def _():
                    self.copy(ref, item, way, axis, target).start()

        def wait_sent():
            for way, (there, target) in enumerate(sends):

                @pl.when(there)
                def _():
                    self.copy(ref, item, way, axis, target).wait_send()

        self.sent.append(wait_sent)

        def from_source():
            @pl.when(jnp.logical_and(active, me == source))
            def _():
                send()

        def elsewhere():
            @pl.when(jnp.logical_and(active, me != source))
            def _():
                self.copy(ref, item, 2, axis, me + 1 - 2 * (me % 2)).wait_recv()
                send()

        return from_source, elsewhere

    def finish(self):
        for wait_sent in self.sent:
            wait_sent()


ITEMS = 48
BLOCKS = LEAD // HB
UPPER = [(i, j) for i in range(BLOCKS) for j in range(i, BLOCKS)]
LEAD_ITEMS = [(0, 1, 0, 0), (1, 1, 0, 0), (2, 2, 0, 1), (4, 1, 0, 0), (5, 2, 0, 1), (7, 3, 1, 1)]


def plan_exchange(ex, n_col, slots, a_ref, b_ref, rows_ref, lead_ref, pan_ref, rhs_ref):
    r, c = ex.r, ex.c
    halves = [pl.ds(0, HB), pl.ds(HB, HB)]
    rows_items = [ex.flow(rows_ref.at[q], "col", q) for q in range(2)]
    lead = []
    for start, count, q, owner in LEAD_ITEMS:
        ref = lead_ref.at[pl.ds(start, count)]
        lead.append((ex.flow(ref, "row", q, active=c == owner), ex.flow(ref, "col", owner)))
    rhs = [
        (ex.flow(rhs_ref.at[q], "row", q, active=c == 2), ex.flow(rhs_ref.at[q], "col", 2))
        for q in range(2)
    ]
    pan = []
    for q in range(2):
        for half in halves:
            for t in range(slots):
                j = c + n_col * t
                active = jnp.logical_and(r >= 2, j >= 2)
                pan.append(ex.flow(pan_ref.at[t, q, half], "row", j, low=2, active=active))

    def start():
        for n, (i, j) in enumerate(UPPER):
            q, owner = i * HB // NB, j * HB // NB

            @pl.when(jnp.logical_and(r == q, c == owner))
            def _():
                lead_ref[n] = a_ref[i * HB % NB : i * HB % NB + HB, j * HB % NB : j * HB % NB + HB]

        for row_flow, _ in lead:
            row_flow[0]()
        for q in range(2):

            @pl.when(c == q)
            def _():
                rows_ref[q] = a_ref[:, :NB]

            rows_items[q][0]()

            @pl.when(jnp.logical_and(r == q, c == 2))
            def _():
                rhs_ref[q] = b_ref[...]

            rhs[q][0][0]()

    def pass_on(pair):
        pair[0][1]()
        pair[1][0]()

    def start_pan():
        for t in range(slots):

            @pl.when(jnp.logical_and(r >= 2, r == c + n_col * t))
            def _():
                pan_ref[t] = rows_ref[...]

        for item in pan:
            item[0]()

    inside = {}

    def put(point, *jobs):
        inside.setdefault(point, []).extend(jobs)

    def along_row(n):
        return lambda: pass_on(lead[n])

    def along_col(n):
        return lead[n][1][1]

    ahead = [start, along_row(0), along_col(0)]
    put(0, along_row(1), along_row(2))
    put(1, along_col(1), along_col(2), rows_items[0][1], rows_items[1][1], start_pan)
    put(2, along_row(3), along_row(4))
    put(3, along_col(3), along_col(4))
    put(4, along_row(5))
    put(5, along_col(5))
    put(6, lambda: pass_on(rhs[0]), lambda: pass_on(rhs[1]))
    put(8, rhs[0][1][1], rhs[1][1][1])
    for n, item in enumerate(pan):
        put(5 + n * 8 // len(pan), item[1])
    return ahead, inside


def rows_of(x, j):
    return jnp.broadcast_to(x[j : j + 1, :], x.shape)


def invert_factor(s):
    sub = lax.broadcasted_iota(jnp.int32, (8, HB), 0)
    lane = lax.broadcasted_iota(jnp.int32, (8, HB), 1)
    groups = len(s)
    t = [jnp.where(lane == sub + 8 * h, 1.0, 0.0).astype(jnp.float32) for h in range(groups)]
    done = []
    for g in range(groups):
        p, q, f = s[g], t[g], t[g]
        lanes = [jnp.broadcast_to(p[:, 8 * g + k : 8 * g + k + 1], (8, HB)) for k in range(8)]
        scale = jnp.ones((8, HB), jnp.float32)
        for j in range(8):
            here = sub == j
            pivot = rows_of(lanes[j], j)
            inv = 1.0 / pivot
            m = lanes[j] * inv
            for k in range(j + 1, 8):
                row = rows_of(lanes[k], j)
                lanes[k] = jnp.where(here, row * inv, lanes[k] - m * row)
            row = rows_of(p, j)
            p = jnp.where(here, row * inv, p - m * row)
            row = rows_of(q, j)
            q = jnp.where(here, row * inv, q - m * row)
            f = jnp.where(sub > j, f - m * rows_of(f, j), f)
            scale = jnp.where(here, pivot, scale)
        root = lax.rsqrt(scale)
        root = root * (1.5 - 0.5 * scale * root * root)
        done.append(f * root)
        if g + 1 < groups:
            prow = [rows_of(p, k) for k in range(8)]
            qrow = [rows_of(q, k) for k in range(8)]
        for h in range(g + 1, groups):
            lane_cols = [
                jnp.broadcast_to(s[h][:, 8 * g + k : 8 * g + k + 1], (8, HB)) for k in range(8)
            ]
            ps = [lane_cols[k] * prow[k] for k in range(8)]
            qs = [lane_cols[k] * qrow[k] for k in range(8)]
            s[h] = s[h] - (((ps[0] + ps[1]) + (ps[2] + ps[3])) + ((ps[4] + ps[5]) + (ps[6] + ps[7])))
            t[h] = t[h] - (((qs[0] + qs[1]) + (qs[2] + qs[3])) + ((qs[4] + qs[5]) + (qs[6] + qs[7])))
    return done


def factor_lead(lead_ref, s_ref, inv_ref):
    blocks = BLOCKS

    def step(kb, carry):
        base = pl.multiple_of(kb * HB, HB)
        for k in range(blocks):

            @pl.when(kb == k)
            def _():
                rows = slice(k * HB, (k + 1) * HB)
                s_ref[rows, rows] += lead_ref[UPPER.index((k, k))]

        groups = [
            s_ref[pl.ds(pl.multiple_of(base + 8 * g, 8), 8), pl.ds(base, HB)] for g in range(HB // 8)
        ]
        li = jnp.concatenate(invert_factor(groups), axis=0)
        inv_ref[pl.ds(base, HB), pl.ds(base, HB)] = li
        for k in range(blocks):

            @pl.when(kb == k)
            def _():
                lo, hi = k * HB, (k + 1) * HB
                if k > 0:
                    inv_ref[lo:hi, :lo] = dot(li, inv_ref[lo:hi, :lo])
                for j in range(k + 1, blocks):
                    s_ref[lo:hi, j * HB : (j + 1) * HB] += lead_ref[UPPER.index((k, j))]
                if k + 1 < blocks:
                    u = dot(li, s_ref[lo:hi, hi:])
                    ut = u.T
                    s_ref[hi:, hi:] -= dot(ut, u)
                    inv_ref[hi:, :hi] -= dot(ut, inv_ref[lo:hi, :hi])

        return carry

    lax.fori_loop(0, blocks, step, 0)


def whole_kernel(
    n_row,
    n_col,
    a_ref,
    b_ref,
    out_ref,
    y_ref,
    rows_ref,
    lead_ref,
    pan_ref,
    rhs_ref,
    s_ref,
    inv_ref,
    send_sem,
    recv_sem,
):
    slots = a_ref.shape[1] // NB
    ex = Exchange(n_row, n_col, send_sem, recv_sem)
    r, c = ex.r, ex.c
    ex.barrier()
    ahead, inside = plan_exchange(
        ex, n_col, slots, a_ref, b_ref, rows_ref, lead_ref, pan_ref, rhs_ref
    )
    ahead[0]()
    s_ref[...] = jnp.zeros_like(s_ref)
    inv_ref[...] = jnp.zeros_like(inv_ref)
    for job in ahead[1:]:
        job()
    for point in sorted(inside):
        for job in inside[point]:
            job()
    factor_lead(lead_ref, s_ref, inv_ref)

    def panel(first, second):
        left = dot_nt(first, inv_ref[:NB, :NB])
        right = dot_nt(first, inv_ref[NB:, :NB]) + dot_nt(second, inv_ref[NB:, NB:])
        return left, right

    p0, p1 = panel(rows_ref[0], rows_ref[1])
    y0 = dot(inv_ref[:NB, :NB], rhs_ref[0])
    y1 = dot(inv_ref[NB:, :NB], rhs_ref[0]) + dot(inv_ref[NB:, NB:], rhs_ref[1])
    updated = b_ref[...] - (dot(p0, y0) + dot(p1, y1))
    y_ref[...] = jnp.where(r == 0, y0, jnp.where(r == 1, y1, updated))
    tri = lax.broadcasted_iota(jnp.int32, (NB, NB), 0) >= lax.broadcasted_iota(jnp.int32, (NB, NB), 1)
    for slot in range(slots):
        cols = slice(slot * NB, (slot + 1) * NB)
        j = c + n_col * slot
        inner = jnp.logical_and(r >= 2, j >= 2)

        @pl.when(inner)
        def _():
            z0, z1 = panel(pan_ref[slot, 0], pan_ref[slot, 1])
            out_ref[:, cols] = a_ref[:, cols] - (dot_nt(p0, z0) + dot_nt(p1, z1))

        @pl.when(jnp.logical_not(inner))
        def _():
            keep = jnp.logical_or(r > j, jnp.logical_and(r == j, tri))
            out_ref[:, cols] = jnp.where(keep, jnp.where(j == 0, p0, p1), 0.0)

    ex.finish()


def whole(n_row, n_col, a, b):
    vmem = pl.BlockSpec(memory_space=pltpu.VMEM)
    shapes = [
        (2, NB, NB),
        (len(UPPER), HB, HB),
        (a.shape[1] // NB, 2, NB, NB),
        (2,) + b.shape,
        (LEAD, LEAD),
        (LEAD, LEAD),
    ]
    return pl.pallas_call(
        functools.partial(whole_kernel, n_row, n_col),
        out_shape=[jax.ShapeDtypeStruct(x.shape, jnp.float32) for x in (a, b)],
        in_specs=[vmem] * 2,
        out_specs=[vmem] * 2,
        scratch_shapes=[pltpu.VMEM(s, jnp.float32) for s in shapes]
        + [pltpu.SemaphoreType.DMA((ITEMS, 3)), pltpu.SemaphoreType.DMA((ITEMS,))],
        compiler_params=pltpu.CompilerParams(
            collective_id=0, has_side_effects=True, vmem_limit_bytes=40 * 1024 * 1024
        ),
    )(a, b)


def solution(mesh):
    n_row, n_col = mesh.shape["row"], mesh.shape["col"]

    def per_device(a, b):
        return tuple(whole(n_row, n_col, a, b))

    placed = (P("row", "col"), P("row", None))
    return jax.shard_map(
        per_device, mesh=mesh, in_specs=placed, out_specs=placed, check_vma=False
    )
```

```python
import functools

import jax
import jax.numpy as jnp
from jax import lax
from jax.experimental import pallas as pl
from jax.experimental.pallas import tpu as pltpu
from jax.sharding import PartitionSpec as P

NB = 256
HB = 128
LEAD = 2 * NB
MESH = pl.DeviceIdType.MESH
highest = lax.Precision.HIGHEST


def dot(a, b):
    return jnp.dot(a, b, precision=highest, preferred_element_type=jnp.float32)


def dot_nt(a, b):
    return lax.dot_general(
        a, b, (((1,), (1,)), ((), ())), precision=highest, preferred_element_type=jnp.float32
    )


class Exchange:
    def __init__(self, n_row, n_col, send_sem, recv_sem):
        self.r = lax.axis_index("row")
        self.c = lax.axis_index("col")
        self.axes = {"row": (self.r, n_row), "col": (self.c, n_col)}
        self.send_sem, self.recv_sem = send_sem, recv_sem
        self.items = 0
        self.sent = []

    def at(self, axis, index):
        return (index, self.c) if axis == "row" else (self.r, index)

    def barrier(self):
        barrier = pltpu.get_barrier_semaphore()
        peers = 0
        for axis, (me, size) in self.axes.items():
            for there, target in (
                (None, me + 1 - 2 * (me % 2)),
                (me + 2 < size, me + 2),
                (me >= 2, me - 2),
            ):

                def signal():
                    pl.semaphore_signal(
                        barrier, inc=1, device_id=self.at(axis, target), device_id_type=MESH
                    )

                if there is None:
                    signal()
                    peers += 1
                else:
                    pl.when(there)(signal)
                    peers += there.astype(jnp.int32)
        pl.semaphore_wait(barrier, peers)

    def copy(self, ref, item, way, axis, target):
        return pltpu.make_async_remote_copy(
            src_ref=ref,
            dst_ref=ref,
            send_sem=self.send_sem.at[item, way],
            recv_sem=self.recv_sem.at[item],
            device_id=self.at(axis, target),
            device_id_type=MESH,
        )

    def flow(self, ref, axis, source, low=0, active=True, cross=False):
        me, size = self.axes[axis]
        root = source + 1 - 2 * (source % 2) if cross else source
        item = self.items
        self.items += 1
        chain = jnp.logical_and(active, me % 2 == root % 2)
        to_pair = jnp.logical_or(me == source, jnp.logical_and(chain, me // 2 != source // 2))
        sends = (
            (jnp.logical_and(chain, jnp.logical_and(me >= root, me + 2 < size)), me + 2),
            (jnp.logical_and(chain, jnp.logical_and(me <= root, me >= low + 2)), me - 2),
            (jnp.logical_and(active, to_pair), me + 1 - 2 * (me % 2)),
        )

        def send():
            for way, (there, target) in enumerate(sends):

                @pl.when(there)
                def _():
                    self.copy(ref, item, way, axis, target).start()

        def wait_sent():
            for way, (there, target) in enumerate(sends):

                @pl.when(there)
                def _():
                    self.copy(ref, item, way, axis, target).wait_send()

        self.sent.append(wait_sent)

        def from_source():
            @pl.when(jnp.logical_and(active, me == source))
            def _():
                send()

        def elsewhere():
            @pl.when(jnp.logical_and(active, me != source))
            def _():
                self.copy(ref, item, 2, axis, me + 1 - 2 * (me % 2)).wait_recv()
                send()

        return from_source, elsewhere

    def finish(self):
        for wait_sent in self.sent:
            wait_sent()


ITEMS = 48
POINTS = 4
BLOCKS = LEAD // HB
UPPER = [(i, j) for i in range(BLOCKS) for j in range(i, BLOCKS)]
LEAD_ITEMS = [(0, 1, 0, 0), (1, 1, 0, 0), (2, 2, 0, 1), (4, 1, 0, 0), (5, 2, 0, 1), (7, 3, 1, 1)]


def plan_exchange(ex, n_col, slots, a_ref, b_ref, rows_ref, lead_ref, pan_ref, rhs_ref):
    r, c = ex.r, ex.c
    halves = [pl.ds(0, HB), pl.ds(HB, HB)]
    rows_early = [ex.flow(rows_ref.at[q], "col", q, active=r >= 2) for q in range(2)]
    rows_late = [ex.flow(rows_ref.at[q], "col", q, active=r < 2) for q in range(2)]
    lead = []
    for start, count, q, owner in LEAD_ITEMS:
        ref = lead_ref.at[pl.ds(start, count)]
        lead.append((ex.flow(ref, "row", q, active=c == owner), ex.flow(ref, "col", owner)))
    rhs = [
        (ex.flow(rhs_ref.at[q], "row", q, active=c == 2), ex.flow(rhs_ref.at[q], "col", 2))
        for q in range(2)
    ]
    pan = []
    for q in range(2):
        for h, half in enumerate(halves):
            for t in range(slots):
                j = c + n_col * t
                active = jnp.logical_and(r >= 2, j >= 2)
                ref = pan_ref.at[t, q, half]
                pan.append(ex.flow(ref, "row", j, low=2, active=active, cross=h == 1))

    def start():
        for n, (i, j) in enumerate(UPPER):
            q, owner = i * HB // NB, j * HB // NB

            @pl.when(jnp.logical_and(r == q, c == owner))
            def _():
                lead_ref[n] = a_ref[i * HB % NB : i * HB % NB + HB, j * HB % NB : j * HB % NB + HB]

        for row_flow, _ in lead:
            row_flow[0]()
        for q in range(2):

            @pl.when(c == q)
            def _():
                rows_ref[q] = a_ref[:, :NB]

            rows_early[q][0]()

            @pl.when(jnp.logical_and(r == q, c == 2))
            def _():
                rhs_ref[q] = b_ref[...]

            rhs[q][0][0]()

    def pass_on(pair):
        pair[0][1]()
        pair[1][0]()

    def start_pan():
        for t in range(slots):

            @pl.when(jnp.logical_and(r >= 2, r == c + n_col * t))
            def _():
                pan_ref[t] = rows_ref[...]

        for item in pan:
            item[0]()

    inside = {}

    def put(point, *jobs):
        inside.setdefault(point, []).extend(jobs)

    def along_row(n):
        return lambda: pass_on(lead[n])

    def along_col(n):
        return lead[n][1][1]

    ahead = [start, along_row(0), along_col(0)]
    put(0, along_row(1), along_row(2))
    put(1, along_col(1), along_col(2), rows_early[0][1], rows_early[1][1], start_pan)
    put(2, along_row(3), along_row(4))
    put(3, along_col(3), along_col(4))
    put(4, along_row(5))
    put(5, along_col(5))
    put(6, lambda: pass_on(rhs[0]), lambda: pass_on(rhs[1]))
    put(8, rhs[0][1][1], rhs[1][1][1])
    put(5, rows_late[0][0], rows_late[1][0])
    put(10, rows_late[0][1], rows_late[1][1])
    for n, item in enumerate(pan):
        put(5 + n * 8 // len(pan), item[1])
    return ahead, inside


def rows_of(x, j):
    return jnp.broadcast_to(x[j : j + 1, :], x.shape)


def invert_factor(s, hook=lambda point: None):
    sub = lax.broadcasted_iota(jnp.int32, (8, HB), 0)
    lane = lax.broadcasted_iota(jnp.int32, (8, HB), 1)
    groups = len(s)
    t = [jnp.where(lane == sub + 8 * h, 1.0, 0.0).astype(jnp.float32) for h in range(groups)]
    done = []
    for g in range(groups):
        if g % (groups // POINTS) == 0:
            hook(g // (groups // POINTS))
        p, q, f = s[g], t[g], t[g]
        lanes = [jnp.broadcast_to(p[:, 8 * g + k : 8 * g + k + 1], (8, HB)) for k in range(8)]
        scale = jnp.ones((8, HB), jnp.float32)
        for j in range(8):
            here = sub == j
            pivot = rows_of(lanes[j], j)
            inv = 1.0 / pivot
            m = lanes[j] * inv
            for k in range(j + 1, 8):
                row = rows_of(lanes[k], j)
                lanes[k] = jnp.where(here, row * inv, lanes[k] - m * row)
            row = rows_of(p, j)
            p = jnp.where(here, row * inv, p - m * row)
            row = rows_of(q, j)
            q = jnp.where(here, row * inv, q - m * row)
            f = jnp.where(sub > j, f - m * rows_of(f, j), f)
            scale = jnp.where(here, pivot, scale)
        root = lax.rsqrt(scale)
        root = root * (1.5 - 0.5 * scale * root * root)
        done.append(f * root)
        if g + 1 < groups:
            prow = [rows_of(p, k) for k in range(8)]
            qrow = [rows_of(q, k) for k in range(8)]
        for h in range(g + 1, groups):
            lane_cols = [
                jnp.broadcast_to(s[h][:, 8 * g + k : 8 * g + k + 1], (8, HB)) for k in range(8)
            ]
            ps = [lane_cols[k] * prow[k] for k in range(8)]
            qs = [lane_cols[k] * qrow[k] for k in range(8)]
            s[h] = s[h] - (((ps[0] + ps[1]) + (ps[2] + ps[3])) + ((ps[4] + ps[5]) + (ps[6] + ps[7])))
            t[h] = t[h] - (((qs[0] + qs[1]) + (qs[2] + qs[3])) + ((qs[4] + qs[5]) + (qs[6] + qs[7])))
    return done


def factor_lead(lead_ref, s_ref, inv_ref, inside):
    blocks = BLOCKS

    def step(kb, carry):
        def hook(point):
            for k in range(blocks):
                jobs = inside.get(k * POINTS + point)
                if jobs:

                    @pl.when(kb == k)
                    def _():
                        for job in jobs:
                            job()

        base = pl.multiple_of(kb * HB, HB)
        for k in range(blocks):

            @pl.when(kb == k)
            def _():
                rows = slice(k * HB, (k + 1) * HB)
                s_ref[rows, rows] += lead_ref[UPPER.index((k, k))]

        groups = [
            s_ref[pl.ds(pl.multiple_of(base + 8 * g, 8), 8), pl.ds(base, HB)] for g in range(HB // 8)
        ]
        li = jnp.concatenate(invert_factor(groups, hook), axis=0)
        inv_ref[pl.ds(base, HB), pl.ds(base, HB)] = li
        for k in range(blocks):

            @pl.when(kb == k)
            def _():
                lo, hi = k * HB, (k + 1) * HB
                if k > 0:
                    inv_ref[lo:hi, :lo] = dot(li, inv_ref[lo:hi, :lo])
                for j in range(k + 1, blocks):
                    s_ref[lo:hi, j * HB : (j + 1) * HB] += lead_ref[UPPER.index((k, j))]
                if k + 1 < blocks:
                    u = dot(li, s_ref[lo:hi, hi:])
                    ut = u.T
                    s_ref[hi:, hi:] -= dot(ut, u)
                    inv_ref[hi:, :hi] -= dot(ut, inv_ref[lo:hi, :hi])

        return carry

    lax.fori_loop(0, blocks, step, 0)


def whole_kernel(
    n_row,
    n_col,
    a_ref,
    b_ref,
    out_ref,
    y_ref,
    rows_ref,
    lead_ref,
    pan_ref,
    rhs_ref,
    s_ref,
    inv_ref,
    send_sem,
    recv_sem,
):
    slots = a_ref.shape[1] // NB
    ex = Exchange(n_row, n_col, send_sem, recv_sem)
    r, c = ex.r, ex.c
    ex.barrier()
    ahead, inside = plan_exchange(
        ex, n_col, slots, a_ref, b_ref, rows_ref, lead_ref, pan_ref, rhs_ref
    )
    ahead[0]()
    s_ref[...] = jnp.zeros_like(s_ref)
    inv_ref[...] = jnp.zeros_like(inv_ref)
    for job in ahead[1:]:
        job()
    factor_lead(lead_ref, s_ref, inv_ref, inside)

    def panel(first, second):
        left = dot_nt(first, inv_ref[:NB, :NB])
        right = dot_nt(first, inv_ref[NB:, :NB]) + dot_nt(second, inv_ref[NB:, NB:])
        return left, right

    p0, p1 = panel(rows_ref[0], rows_ref[1])
    y0 = dot(inv_ref[:NB, :NB], rhs_ref[0])
    y1 = dot(inv_ref[NB:, :NB], rhs_ref[0]) + dot(inv_ref[NB:, NB:], rhs_ref[1])
    updated = b_ref[...] - (dot(p0, y0) + dot(p1, y1))
    y_ref[...] = jnp.where(r == 0, y0, jnp.where(r == 1, y1, updated))
    tri = lax.broadcasted_iota(jnp.int32, (NB, NB), 0) >= lax.broadcasted_iota(jnp.int32, (NB, NB), 1)
    for slot in range(slots):
        cols = slice(slot * NB, (slot + 1) * NB)
        j = c + n_col * slot
        inner = jnp.logical_and(r >= 2, j >= 2)

        @pl.when(inner)
        def _():
            z0, z1 = panel(pan_ref[slot, 0], pan_ref[slot, 1])
            out_ref[:, cols] = a_ref[:, cols] - (dot_nt(p0, z0) + dot_nt(p1, z1))

        @pl.when(jnp.logical_not(inner))
        def _():
            keep = jnp.logical_or(r > j, jnp.logical_and(r == j, tri))
            out_ref[:, cols] = jnp.where(keep, jnp.where(j == 0, p0, p1), 0.0)

    ex.finish()


def whole(n_row, n_col, a, b):
    vmem = pl.BlockSpec(memory_space=pltpu.VMEM)
    shapes = [
        (2, NB, NB),
        (len(UPPER), HB, HB),
        (a.shape[1] // NB, 2, NB, NB),
        (2,) + b.shape,
        (LEAD, LEAD),
        (LEAD, LEAD),
    ]
    return pl.pallas_call(
        functools.partial(whole_kernel, n_row, n_col),
        out_shape=[jax.ShapeDtypeStruct(x.shape, jnp.float32) for x in (a, b)],
        in_specs=[vmem] * 2,
        out_specs=[vmem] * 2,
        scratch_shapes=[pltpu.VMEM(s, jnp.float32) for s in shapes]
        + [pltpu.SemaphoreType.DMA((ITEMS, 3)), pltpu.SemaphoreType.DMA((ITEMS,))],
        compiler_params=pltpu.CompilerParams(
            collective_id=0, has_side_effects=True, vmem_limit_bytes=40 * 1024 * 1024
        ),
    )(a, b)


def solution(mesh):
    n_row, n_col = mesh.shape["row"], mesh.shape["col"]

    def per_device(a, b):
        return tuple(whole(n_row, n_col, a, b))

    placed = (P("row", "col"), P("row", None))
    return jax.shard_map(
        per_device, mesh=mesh, in_specs=placed, out_specs=placed, check_vma=False
    )
```

```python
import functools

import jax
import jax.numpy as jnp
from jax import lax
from jax.experimental import pallas as pl
from jax.experimental.pallas import tpu as pltpu
from jax.sharding import PartitionSpec as P

NB = 256
HB = 128
LEAD = 2 * NB
MESH = pl.DeviceIdType.MESH
highest = lax.Precision.HIGHEST


def dot(a, b):
    return jnp.dot(a, b, precision=highest, preferred_element_type=jnp.float32)


def dot_nt(a, b):
    return lax.dot_general(
        a, b, (((1,), (1,)), ((), ())), precision=highest, preferred_element_type=jnp.float32
    )


class Exchange:
    def __init__(self, n_row, n_col, send_sem, recv_sem):
        self.r = lax.axis_index("row")
        self.c = lax.axis_index("col")
        self.axes = {"row": (self.r, n_row), "col": (self.c, n_col)}
        self.send_sem, self.recv_sem = send_sem, recv_sem
        self.items = 0
        self.sent = []

    def at(self, axis, index):
        return (index, self.c) if axis == "row" else (self.r, index)

    def barrier(self):
        barrier = pltpu.get_barrier_semaphore()
        peers = 0
        for axis, (me, size) in self.axes.items():
            for there, target in (
                (None, me + 1 - 2 * (me % 2)),
                (me + 2 < size, me + 2),
                (me >= 2, me - 2),
                (me + 4 < size, me + 4),
                (me >= 4, me - 4),
            ):

                def signal():
                    pl.semaphore_signal(
                        barrier, inc=1, device_id=self.at(axis, target), device_id_type=MESH
                    )

                if there is None:
                    signal()
                    peers += 1
                else:
                    pl.when(there)(signal)
                    peers += there.astype(jnp.int32)
        pl.semaphore_wait(barrier, peers)

    def copy(self, ref, item, way, axis, target):
        return pltpu.make_async_remote_copy(
            src_ref=ref,
            dst_ref=ref,
            send_sem=self.send_sem.at[item, way],
            recv_sem=self.recv_sem.at[item],
            device_id=self.at(axis, target),
            device_id_type=MESH,
        )

    def flow(self, ref, axis, source, low=0, active=True, far=False):
        me, size = self.axes[axis]
        item = self.items
        self.items += 1
        chain = jnp.logical_and(active, me % 2 == source % 2)
        up = jnp.logical_and(chain, me >= source)
        down = jnp.logical_and(chain, me <= source)
        ahead = []
        if far:
            relay = (me // 2 + source // 2) % 2 == 0
            up, down = jnp.logical_and(up, relay), jnp.logical_and(down, relay)
            ahead = [
                (jnp.logical_and(up, me + 4 < size), me + 4),
                (jnp.logical_and(down, me >= low + 4), me - 4),
            ]
        sends = ahead + [
            (jnp.logical_and(up, me + 2 < size), me + 2),
            (jnp.logical_and(down, me >= low + 2), me - 2),
            (chain, me + 1 - 2 * (me % 2)),
        ]

        def send():
            for way, (there, target) in enumerate(sends):

                @pl.when(there)
                def _():
                    self.copy(ref, item, way, axis, target).start()

        def wait_sent():
            for way, (there, target) in enumerate(sends):

                @pl.when(there)
                def _():
                    self.copy(ref, item, way, axis, target).wait_send()

        self.sent.append(wait_sent)

        def from_source():
            @pl.when(jnp.logical_and(active, me == source))
            def _():
                send()

        def elsewhere():
            @pl.when(jnp.logical_and(active, me != source))
            def _():
                self.copy(ref, item, 2, axis, me + 1 - 2 * (me % 2)).wait_recv()
                send()

        return from_source, elsewhere

    def finish(self):
        for wait_sent in self.sent:
            wait_sent()


ITEMS = 48
POINTS = 4
BLOCKS = LEAD // HB
UPPER = [(i, j) for i in range(BLOCKS) for j in range(i, BLOCKS)]
LEAD_ITEMS = [(0, 1, 0, 0), (1, 1, 0, 0), (2, 2, 0, 1), (4, 1, 0, 0), (5, 2, 0, 1), (7, 3, 1, 1)]


def plan_exchange(ex, n_col, slots, a_ref, b_ref, rows_ref, lead_ref, pan_ref, rhs_ref):
    r, c = ex.r, ex.c
    halves = [pl.ds(0, HB), pl.ds(HB, HB)]
    rows_early = [ex.flow(rows_ref.at[q], "col", q, active=r >= 2) for q in range(2)]
    rows_late = [ex.flow(rows_ref.at[q], "col", q, active=r < 2) for q in range(2)]
    lead = []
    for start, count, q, owner in LEAD_ITEMS:
        ref = lead_ref.at[pl.ds(start, count)]
        lead.append((ex.flow(ref, "row", q, active=c == owner), ex.flow(ref, "col", owner)))
    rhs = [
        (ex.flow(rhs_ref.at[q], "row", q, active=c == 2), ex.flow(rhs_ref.at[q], "col", 2))
        for q in range(2)
    ]
    pan = []
    for q in range(2):
        for half in halves:
            for t in range(slots):
                j = c + n_col * t
                active = jnp.logical_and(r >= 2, j >= 2)
                pan.append(ex.flow(pan_ref.at[t, q, half], "row", j, low=2, active=active, far=True))

    def start():
        for n, (i, j) in enumerate(UPPER):
            q, owner = i * HB // NB, j * HB // NB

            @pl.when(jnp.logical_and(r == q, c == owner))
            def _():
                lead_ref[n] = a_ref[i * HB % NB : i * HB % NB + HB, j * HB % NB : j * HB % NB + HB]

        for row_flow, _ in lead:
            row_flow[0]()
        for q in range(2):

            @pl.when(c == q)
            def _():
                rows_ref[q] = a_ref[:, :NB]

            rows_early[q][0]()

            @pl.when(jnp.logical_and(r == q, c == 2))
            def _():
                rhs_ref[q] = b_ref[...]

            rhs[q][0][0]()

    def pass_on(pair):
        pair[0][1]()
        pair[1][0]()

    def start_pan():
        for t in range(slots):

            @pl.when(jnp.logical_and(r >= 2, r == c + n_col * t))
            def _():
                pan_ref[t] = rows_ref[...]

        for item in pan:
            item[0]()

    inside = {}

    def put(point, *jobs):
        inside.setdefault(point, []).extend(jobs)

    def along_row(n):
        return lambda: pass_on(lead[n])

    def along_col(n):
        return lead[n][1][1]

    ahead = [start, along_row(0), along_col(0)]
    put(0, along_row(1), along_row(2))
    put(1, along_col(1), along_col(2), rows_early[0][1], rows_early[1][1], start_pan)
    put(2, along_row(3), along_row(4))
    put(3, along_col(3), along_col(4))
    put(4, along_row(5))
    put(5, along_col(5))
    put(6, lambda: pass_on(rhs[0]), lambda: pass_on(rhs[1]))
    put(8, rhs[0][1][1], rhs[1][1][1])
    put(5, rows_late[0][0], rows_late[1][0])
    put(10, rows_late[0][1], rows_late[1][1])
    for n, item in enumerate(pan):
        put(5 + n * 8 // len(pan), item[1])
    return ahead, inside


def rows_of(x, j):
    return jnp.broadcast_to(x[j : j + 1, :], x.shape)


def invert_factor(s, hook=lambda point: None):
    sub = lax.broadcasted_iota(jnp.int32, (8, HB), 0)
    lane = lax.broadcasted_iota(jnp.int32, (8, HB), 1)
    groups = len(s)
    t = [jnp.where(lane == sub + 8 * h, 1.0, 0.0).astype(jnp.float32) for h in range(groups)]
    done = []
    for g in range(groups):
        if g % (groups // POINTS) == 0:
            hook(g // (groups // POINTS))
        p, q, f = s[g], t[g], t[g]
        lanes = [jnp.broadcast_to(p[:, 8 * g + k : 8 * g + k + 1], (8, HB)) for k in range(8)]
        scale = jnp.ones((8, HB), jnp.float32)
        for j in range(8):
            here = sub == j
            pivot = rows_of(lanes[j], j)
            inv = 1.0 / pivot
            m = lanes[j] * inv
            for k in range(j + 1, 8):
                row = rows_of(lanes[k], j)
                lanes[k] = jnp.where(here, row * inv, lanes[k] - m * row)
            row = rows_of(p, j)
            p = jnp.where(here, row * inv, p - m * row)
            row = rows_of(q, j)
            q = jnp.where(here, row * inv, q - m * row)
            f = jnp.where(sub > j, f - m * rows_of(f, j), f)
            scale = jnp.where(here, pivot, scale)
        root = lax.rsqrt(scale)
        root = root * (1.5 - 0.5 * scale * root * root)
        done.append(f * root)
        if g + 1 < groups:
            prow = [rows_of(p, k) for k in range(8)]
            qrow = [rows_of(q, k) for k in range(8)]
        for h in range(g + 1, groups):
            lane_cols = [
                jnp.broadcast_to(s[h][:, 8 * g + k : 8 * g + k + 1], (8, HB)) for k in range(8)
            ]
            ps = [lane_cols[k] * prow[k] for k in range(8)]
            qs = [lane_cols[k] * qrow[k] for k in range(8)]
            s[h] = s[h] - (((ps[0] + ps[1]) + (ps[2] + ps[3])) + ((ps[4] + ps[5]) + (ps[6] + ps[7])))
            t[h] = t[h] - (((qs[0] + qs[1]) + (qs[2] + qs[3])) + ((qs[4] + qs[5]) + (qs[6] + qs[7])))
    return done


def factor_lead(lead_ref, s_ref, inv_ref, inside):
    blocks = BLOCKS

    def step(kb, carry):
        def hook(point):
            for k in range(blocks):
                jobs = inside.get(k * POINTS + point)
                if jobs:

                    @pl.when(kb == k)
                    def _():
                        for job in jobs:
                            job()

        base = pl.multiple_of(kb * HB, HB)
        for k in range(blocks):

            @pl.when(kb == k)
            def _():
                rows = slice(k * HB, (k + 1) * HB)
                s_ref[rows, rows] += lead_ref[UPPER.index((k, k))]

        groups = [
            s_ref[pl.ds(pl.multiple_of(base + 8 * g, 8), 8), pl.ds(base, HB)] for g in range(HB // 8)
        ]
        li = jnp.concatenate(invert_factor(groups, hook), axis=0)
        inv_ref[pl.ds(base, HB), pl.ds(base, HB)] = li
        for k in range(blocks):

            @pl.when(kb == k)
            def _():
                lo, hi = k * HB, (k + 1) * HB
                if k > 0:
                    inv_ref[lo:hi, :lo] = dot(li, inv_ref[lo:hi, :lo])
                for j in range(k + 1, blocks):
                    s_ref[lo:hi, j * HB : (j + 1) * HB] += lead_ref[UPPER.index((k, j))]
                if k + 1 < blocks:
                    u = dot(li, s_ref[lo:hi, hi:])
                    ut = u.T
                    s_ref[hi:, hi:] -= dot(ut, u)
                    inv_ref[hi:, :hi] -= dot(ut, inv_ref[lo:hi, :hi])

        return carry

    lax.fori_loop(0, blocks, step, 0)


def whole_kernel(
    n_row,
    n_col,
    a_ref,
    b_ref,
    out_ref,
    y_ref,
    rows_ref,
    lead_ref,
    pan_ref,
    rhs_ref,
    s_ref,
    inv_ref,
    send_sem,
    recv_sem,
):
    slots = a_ref.shape[1] // NB
    ex = Exchange(n_row, n_col, send_sem, recv_sem)
    r, c = ex.r, ex.c
    ex.barrier()
    ahead, inside = plan_exchange(
        ex, n_col, slots, a_ref, b_ref, rows_ref, lead_ref, pan_ref, rhs_ref
    )
    ahead[0]()
    s_ref[...] = jnp.zeros_like(s_ref)
    inv_ref[...] = jnp.zeros_like(inv_ref)
    for job in ahead[1:]:
        job()
    factor_lead(lead_ref, s_ref, inv_ref, inside)

    def panel(first, second):
        left = dot_nt(first, inv_ref[:NB, :NB])
        right = dot_nt(first, inv_ref[NB:, :NB]) + dot_nt(second, inv_ref[NB:, NB:])
        return left, right

    p0, p1 = panel(rows_ref[0], rows_ref[1])
    y0 = dot(inv_ref[:NB, :NB], rhs_ref[0])
    y1 = dot(inv_ref[NB:, :NB], rhs_ref[0]) + dot(inv_ref[NB:, NB:], rhs_ref[1])
    updated = b_ref[...] - (dot(p0, y0) + dot(p1, y1))
    y_ref[...] = jnp.where(r == 0, y0, jnp.where(r == 1, y1, updated))
    tri = lax.broadcasted_iota(jnp.int32, (NB, NB), 0) >= lax.broadcasted_iota(jnp.int32, (NB, NB), 1)
    for slot in range(slots):
        cols = slice(slot * NB, (slot + 1) * NB)
        j = c + n_col * slot
        inner = jnp.logical_and(r >= 2, j >= 2)

        @pl.when(inner)
        def _():
            z0, z1 = panel(pan_ref[slot, 0], pan_ref[slot, 1])
            out_ref[:, cols] = a_ref[:, cols] - (dot_nt(p0, z0) + dot_nt(p1, z1))

        @pl.when(jnp.logical_not(inner))
        def _():
            keep = jnp.logical_or(r > j, jnp.logical_and(r == j, tri))
            out_ref[:, cols] = jnp.where(keep, jnp.where(j == 0, p0, p1), 0.0)

    ex.finish()


def whole(n_row, n_col, a, b):
    vmem = pl.BlockSpec(memory_space=pltpu.VMEM)
    shapes = [
        (2, NB, NB),
        (len(UPPER), HB, HB),
        (a.shape[1] // NB, 2, NB, NB),
        (2,) + b.shape,
        (LEAD, LEAD),
        (LEAD, LEAD),
    ]
    return pl.pallas_call(
        functools.partial(whole_kernel, n_row, n_col),
        out_shape=[jax.ShapeDtypeStruct(x.shape, jnp.float32) for x in (a, b)],
        in_specs=[vmem] * 2,
        out_specs=[vmem] * 2,
        scratch_shapes=[pltpu.VMEM(s, jnp.float32) for s in shapes]
        + [pltpu.SemaphoreType.DMA((ITEMS, 5)), pltpu.SemaphoreType.DMA((ITEMS,))],
        compiler_params=pltpu.CompilerParams(
            collective_id=0, has_side_effects=True, vmem_limit_bytes=40 * 1024 * 1024
        ),
    )(a, b)


def solution(mesh):
    n_row, n_col = mesh.shape["row"], mesh.shape["col"]

    def per_device(a, b):
        return tuple(whole(n_row, n_col, a, b))

    placed = (P("row", "col"), P("row", None))
    return jax.shard_map(
        per_device, mesh=mesh, in_specs=placed, out_specs=placed, check_vma=False
    )
```

```python
import functools

import jax
import jax.numpy as jnp
from jax import lax
from jax.experimental import pallas as pl
from jax.experimental.pallas import tpu as pltpu
from jax.sharding import PartitionSpec as P

NB = 256
HB = 128
LEAD = 2 * NB
MESH = pl.DeviceIdType.MESH
highest = lax.Precision.HIGHEST


def dot(a, b):
    return jnp.dot(a, b, precision=highest, preferred_element_type=jnp.float32)


def dot_nt(a, b):
    return lax.dot_general(
        a, b, (((1,), (1,)), ((), ())), precision=highest, preferred_element_type=jnp.float32
    )


class Exchange:
    def __init__(self, n_row, n_col, send_sem, recv_sem):
        self.r = lax.axis_index("row")
        self.c = lax.axis_index("col")
        self.axes = {"row": (self.r, n_row), "col": (self.c, n_col)}
        self.send_sem, self.recv_sem = send_sem, recv_sem
        self.items = 0
        self.sent = []

    def at(self, axis, index):
        return (index, self.c) if axis == "row" else (self.r, index)

    def barrier(self):
        barrier = pltpu.get_barrier_semaphore()
        peers = 0
        for axis, (me, size) in self.axes.items():
            for there, target in (
                (None, me + 1 - 2 * (me % 2)),
                (me + 2 < size, me + 2),
                (me >= 2, me - 2),
                (me + 4 < size, me + 4),
                (me >= 4, me - 4),
            ):

                def signal():
                    pl.semaphore_signal(
                        barrier, inc=1, device_id=self.at(axis, target), device_id_type=MESH
                    )

                if there is None:
                    signal()
                    peers += 1
                else:
                    pl.when(there)(signal)
                    peers += there.astype(jnp.int32)
        pl.semaphore_wait(barrier, peers)

    def copy(self, ref, item, way, axis, target):
        return pltpu.make_async_remote_copy(
            src_ref=ref,
            dst_ref=ref,
            send_sem=self.send_sem.at[item, way],
            recv_sem=self.recv_sem.at[item],
            device_id=self.at(axis, target),
            device_id_type=MESH,
        )

    def flow(self, ref, axis, source, low=0, active=True, far=False):
        me, size = self.axes[axis]
        item = self.items
        self.items += 1
        chain = jnp.logical_and(active, me % 2 == source % 2)
        up = jnp.logical_and(chain, me >= source)
        down = jnp.logical_and(chain, me <= source)
        ahead = []
        if far:
            relay = (me // 2 + source // 2) % 2 == 0
            up, down = jnp.logical_and(up, relay), jnp.logical_and(down, relay)
            ahead = [
                (jnp.logical_and(up, me + 4 < size), me + 4),
                (jnp.logical_and(down, me >= low + 4), me - 4),
            ]
        sends = ahead + [
            (jnp.logical_and(up, me + 2 < size), me + 2),
            (jnp.logical_and(down, me >= low + 2), me - 2),
            (chain, me + 1 - 2 * (me % 2)),
        ]

        def send():
            for way, (there, target) in enumerate(sends):

                @pl.when(there)
                def _():
                    self.copy(ref, item, way, axis, target).start()

        def wait_sent():
            for way, (there, target) in enumerate(sends):

                @pl.when(there)
                def _():
                    self.copy(ref, item, way, axis, target).wait_send()

        self.sent.append(wait_sent)

        def from_source():
            @pl.when(jnp.logical_and(active, me == source))
            def _():
                send()

        def elsewhere():
            @pl.when(jnp.logical_and(active, me != source))
            def _():
                self.copy(ref, item, 2, axis, me + 1 - 2 * (me % 2)).wait_recv()
                send()

        return from_source, elsewhere

    def finish(self):
        for wait_sent in self.sent:
            wait_sent()


ITEMS = 48
POINTS = 4
BLOCKS = LEAD // HB
UPPER = [(i, j) for i in range(BLOCKS) for j in range(i, BLOCKS)]
LEAD_ITEMS = [(0, 1, 0, 0), (1, 1, 0, 0), (2, 2, 0, 1), (4, 1, 0, 0), (5, 2, 0, 1), (7, 3, 1, 1)]


def plan_exchange(ex, n_col, slots, a_ref, b_ref, rows_ref, lead_ref, pan_ref, rhs_ref):
    r, c = ex.r, ex.c
    halves = [pl.ds(0, HB), pl.ds(HB, HB)]
    rows_early = [ex.flow(rows_ref.at[q], "col", q, active=r >= 2) for q in range(2)]
    rows_late = [ex.flow(rows_ref.at[q], "col", q, active=r < 2) for q in range(2)]
    lead = []
    for start, count, q, owner in LEAD_ITEMS:
        ref = lead_ref.at[pl.ds(start, count)]
        lead.append((ex.flow(ref, "row", q, active=c == owner), ex.flow(ref, "col", owner)))
    rhs = [
        (ex.flow(rhs_ref.at[q], "row", q, active=c == 2), ex.flow(rhs_ref.at[q], "col", 2))
        for q in range(2)
    ]
    pan = []
    for q in range(2):
        for half in halves:
            for t in range(slots):
                j = c + n_col * t
                active = jnp.logical_and(r >= 2, j >= 2)
                pan.append(ex.flow(pan_ref.at[t, q, half], "row", j, low=2, active=active, far=True))

    def start():
        for n, (i, j) in enumerate(UPPER):
            q, owner = i * HB // NB, j * HB // NB

            @pl.when(jnp.logical_and(r == q, c == owner))
            def _():
                lead_ref[n] = a_ref[i * HB % NB : i * HB % NB + HB, j * HB % NB : j * HB % NB + HB]

        for row_flow, _ in lead:
            row_flow[0]()
        for q in range(2):

            @pl.when(c == q)
            def _():
                rows_ref[q] = a_ref[:, :NB]

            @pl.when(jnp.logical_and(r == q, c == 2))
            def _():
                rhs_ref[q] = b_ref[...]

            rhs[q][0][0]()

    def pass_on(pair):
        pair[0][1]()
        pair[1][0]()

    def start_pan():
        for t in range(slots):

            @pl.when(jnp.logical_and(r >= 2, r == c + n_col * t))
            def _():
                pan_ref[t] = rows_ref[...]

        for item in pan:
            item[0]()

    inside = {}

    def put(point, *jobs):
        inside.setdefault(point, []).extend(jobs)

    def along_row(n):
        return lambda: pass_on(lead[n])

    def along_col(n):
        return lead[n][1][1]

    ahead = [start, along_row(0), along_col(0)]
    put(0, along_row(1), along_row(2), rows_early[0][0], rows_early[1][0])
    put(1, along_col(1), along_col(2), along_row(3), along_row(4))
    put(2, along_col(3), along_col(4), along_row(5))
    put(4, along_col(5))
    put(5, rows_early[0][1], rows_early[1][1], start_pan, rows_late[0][0], rows_late[1][0])
    put(6, lambda: pass_on(rhs[0]), lambda: pass_on(rhs[1]))
    put(8, rhs[0][1][1], rhs[1][1][1])
    put(10, rows_late[0][1], rows_late[1][1])
    for n, item in enumerate(pan):
        put(8 + n * 8 // len(pan), item[1])
    return ahead, inside


def rows_of(x, j):
    return jnp.broadcast_to(x[j : j + 1, :], x.shape)


def invert_factor(s, hook=lambda point: None):
    sub = lax.broadcasted_iota(jnp.int32, (8, HB), 0)
    lane = lax.broadcasted_iota(jnp.int32, (8, HB), 1)
    groups = len(s)
    t = [jnp.where(lane == sub + 8 * h, 1.0, 0.0).astype(jnp.float32) for h in range(groups)]
    done = []
    for g in range(groups):
        if g % (groups // POINTS) == 0:
            hook(g // (groups // POINTS))
        p, q, f = s[g], t[g], t[g]
        lanes = [jnp.broadcast_to(p[:, 8 * g + k : 8 * g + k + 1], (8, HB)) for k in range(8)]
        scale = jnp.ones((8, HB), jnp.float32)
        for j in range(8):
            here = sub == j
            pivot = rows_of(lanes[j], j)
            inv = 1.0 / pivot
            m = lanes[j] * inv
            for k in range(j + 1, 8):
                row = rows_of(lanes[k], j)
                lanes[k] = jnp.where(here, row * inv, lanes[k] - m * row)
            row = rows_of(p, j)
            p = jnp.where(here, row * inv, p - m * row)
            row = rows_of(q, j)
            q = jnp.where(here, row * inv, q - m * row)
            f = jnp.where(sub > j, f - m * rows_of(f, j), f)
            scale = jnp.where(here, pivot, scale)
        root = lax.rsqrt(scale)
        root = root * (1.5 - 0.5 * scale * root * root)
        done.append(f * root)
        if g + 1 < groups:
            prow = [rows_of(p, k) for k in range(8)]
            qrow = [rows_of(q, k) for k in range(8)]
        for h in range(g + 1, groups):
            lane_cols = [
                jnp.broadcast_to(s[h][:, 8 * g + k : 8 * g + k + 1], (8, HB)) for k in range(8)
            ]
            ps = [lane_cols[k] * prow[k] for k in range(8)]
            qs = [lane_cols[k] * qrow[k] for k in range(8)]
            s[h] = s[h] - (((ps[0] + ps[1]) + (ps[2] + ps[3])) + ((ps[4] + ps[5]) + (ps[6] + ps[7])))
            t[h] = t[h] - (((qs[0] + qs[1]) + (qs[2] + qs[3])) + ((qs[4] + qs[5]) + (qs[6] + qs[7])))
    return done


def factor_lead(lead_ref, s_ref, inv_ref, inside):
    blocks = BLOCKS

    def step(kb, carry):
        def hook(point):
            for k in range(blocks):
                jobs = inside.get(k * POINTS + point)
                if jobs:

                    @pl.when(kb == k)
                    def _():
                        for job in jobs:
                            job()

        base = pl.multiple_of(kb * HB, HB)
        for k in range(blocks):

            @pl.when(kb == k)
            def _():
                rows = slice(k * HB, (k + 1) * HB)
                s_ref[rows, rows] += lead_ref[UPPER.index((k, k))]

        groups = [
            s_ref[pl.ds(pl.multiple_of(base + 8 * g, 8), 8), pl.ds(base, HB)] for g in range(HB // 8)
        ]
        li = jnp.concatenate(invert_factor(groups, hook), axis=0)
        inv_ref[pl.ds(base, HB), pl.ds(base, HB)] = li
        for k in range(blocks):

            @pl.when(kb == k)
            def _():
                lo, hi = k * HB, (k + 1) * HB
                if k > 0:
                    inv_ref[lo:hi, :lo] = dot(li, inv_ref[lo:hi, :lo])
                for j in range(k + 1, blocks):
                    s_ref[lo:hi, j * HB : (j + 1) * HB] += lead_ref[UPPER.index((k, j))]
                if k + 1 < blocks:
                    u = dot(li, s_ref[lo:hi, hi:])
                    ut = u.T
                    s_ref[hi:, hi:] -= dot(ut, u)
                    inv_ref[hi:, :hi] -= dot(ut, inv_ref[lo:hi, :hi])

        return carry

    lax.fori_loop(0, blocks, step, 0)


def whole_kernel(
    n_row,
    n_col,
    a_ref,
    b_ref,
    out_ref,
    y_ref,
    rows_ref,
    lead_ref,
    pan_ref,
    rhs_ref,
    s_ref,
    inv_ref,
    send_sem,
    recv_sem,
):
    slots = a_ref.shape[1] // NB
    ex = Exchange(n_row, n_col, send_sem, recv_sem)
    r, c = ex.r, ex.c
    ex.barrier()
    ahead, inside = plan_exchange(
        ex, n_col, slots, a_ref, b_ref, rows_ref, lead_ref, pan_ref, rhs_ref
    )
    ahead[0]()
    s_ref[...] = jnp.zeros_like(s_ref)
    inv_ref[...] = jnp.zeros_like(inv_ref)
    for job in ahead[1:]:
        job()
    factor_lead(lead_ref, s_ref, inv_ref, inside)

    def panel(first, second):
        left = dot_nt(first, inv_ref[:NB, :NB])
        right = dot_nt(first, inv_ref[NB:, :NB]) + dot_nt(second, inv_ref[NB:, NB:])
        return left, right

    p0, p1 = panel(rows_ref[0], rows_ref[1])
    y0 = dot(inv_ref[:NB, :NB], rhs_ref[0])
    y1 = dot(inv_ref[NB:, :NB], rhs_ref[0]) + dot(inv_ref[NB:, NB:], rhs_ref[1])
    updated = b_ref[...] - (dot(p0, y0) + dot(p1, y1))
    y_ref[...] = jnp.where(r == 0, y0, jnp.where(r == 1, y1, updated))
    tri = lax.broadcasted_iota(jnp.int32, (NB, NB), 0) >= lax.broadcasted_iota(jnp.int32, (NB, NB), 1)
    for slot in range(slots):
        cols = slice(slot * NB, (slot + 1) * NB)
        j = c + n_col * slot
        inner = jnp.logical_and(r >= 2, j >= 2)

        @pl.when(inner)
        def _():
            z0, z1 = panel(pan_ref[slot, 0], pan_ref[slot, 1])
            out_ref[:, cols] = a_ref[:, cols] - (dot_nt(p0, z0) + dot_nt(p1, z1))

        @pl.when(jnp.logical_not(inner))
        def _():
            keep = jnp.logical_or(r > j, jnp.logical_and(r == j, tri))
            out_ref[:, cols] = jnp.where(keep, jnp.where(j == 0, p0, p1), 0.0)

    ex.finish()


def whole(n_row, n_col, a, b):
    vmem = pl.BlockSpec(memory_space=pltpu.VMEM)
    shapes = [
        (2, NB, NB),
        (len(UPPER), HB, HB),
        (a.shape[1] // NB, 2, NB, NB),
        (2,) + b.shape,
        (LEAD, LEAD),
        (LEAD, LEAD),
    ]
    return pl.pallas_call(
        functools.partial(whole_kernel, n_row, n_col),
        out_shape=[jax.ShapeDtypeStruct(x.shape, jnp.float32) for x in (a, b)],
        in_specs=[vmem] * 2,
        out_specs=[vmem] * 2,
        scratch_shapes=[pltpu.VMEM(s, jnp.float32) for s in shapes]
        + [pltpu.SemaphoreType.DMA((ITEMS, 5)), pltpu.SemaphoreType.DMA((ITEMS,))],
        compiler_params=pltpu.CompilerParams(
            collective_id=0, has_side_effects=True, vmem_limit_bytes=40 * 1024 * 1024
        ),
    )(a, b)


def solution(mesh):
    n_row, n_col = mesh.shape["row"], mesh.shape["col"]

    def per_device(a, b):
        return tuple(whole(n_row, n_col, a, b))

    placed = (P("row", "col"), P("row", None))
    return jax.shard_map(
        per_device, mesh=mesh, in_specs=placed, out_specs=placed, check_vma=False
    )
```
